256 devices in a mesh: depth: 4 (over x), col: 64 (over z, y, core).
Axes of the slice: x: 4, y: 4, z: 8, core: 2. Of those that a mesh axis runs over, the one named last changes fastest.
Arguments:
- raw_views: bfloat16 [8, 32, 8, 8192], P('depth', None, None, 'col'), may hold values from -48 to 48
- feat_weight: bfloat16 [9, 32, 32], replicated, may hold values from -0.375 to 0.375
- shifts: int32 [8, 96], replicated, may hold values from 0 to 127, as said below
- frame_range: int32 [8, 2], replicated, may hold values from 0 to 8192, as said below
- cost_weight: bfloat16 [27, 8, 32], replicated, may hold values from -0.21875 to 0.21875
- mid_weight: bfloat16 [27, 8, 8], replicated, may hold values from -0.4375 to 0.4375
- final_weight: bfloat16 [27, 8], replicated, may hold values from -17 to 17
Outputs:
- estimate: float32 [8, 8192], P(None, 'col')
The draws below stay inside these ranges and needn't reach their ends.
Inputs may be any that keep to these rules, and one draw needn't show every extreme that they name: `shifts`: shifts of view 0 are all zero; the largest shift is exactly 127. `frame_range`: row v holds the first and one past the last valid column of view v, the first below the second; view 0 is valid over all 8192 columns.
All inputs are finite; a program needn't handle non-finite values.
Results may differ from the reference program's by a relative error of at most 0.007.
The reference program's roundings to bfloat16 on the way (of `features`, `volume`, `first_act` and `second_act`) count: a program that leaves them out, or rounds other values in their place, can miss the bound.
Values may be sent and summed in bfloat16 or wider, within the bound.
No kernel may reach another device: no remote copies, remote signals or barrier semaphores. Data moves between devices by JAX's collectives and lax.ppermute only.
A program may use at most 64 MiB of HBM per device.

```python
import math
import jax
import jax.numpy as jnp
from jax import lax

V = 8
C = 32
CONV = 8
DEPTHS = 96
ROWS = 8
W = 8192
SMAX = 127


def draw_raw_views(key, part):
    key_one, key_two = jax.random.split(jax.random.fold_in(key, 3), 2)
    column_ids = jnp.arange(W, dtype=jnp.int32)
    columns = column_ids.astype(jnp.float32) / W
    basic_draw = jnp.clip(jax.random.normal(key_one, (V, C, ROWS, W), jnp.float32), -4.0, 4.0)
    col_scale = jnp.exp(math.log(3.0) * columns + jax.random.uniform(key_two, (W,), jnp.float32, 0.0, math.log(4.0)))
    values = basic_draw * col_scale
    return values.astype(jnp.bfloat16)


def draw_shifts(key, part):
    key_one, key_two, key_three = jax.random.split(jax.random.fold_in(key, 11), 3)
    baseline = jax.random.randint(key_one, (V,), SMAX // 2, SMAX + 1)
    forced = jax.random.randint(key_two, (), 1, V)
    views = jnp.arange(V, dtype=jnp.int32)
    baseline = jnp.where(views == forced, SMAX, baseline)
    jitter = jax.random.randint(key_three, (V, DEPTHS), 0, DEPTHS - 1)
    depth_index = jnp.arange(DEPTHS, dtype=jnp.int32)
    result = (depth_index[None, :] * baseline[:, None] + jitter) // (DEPTHS - 1)
    return jnp.where(views[:, None] == 0, 0, result).astype(jnp.int32)


def draw_frame_range(key, part):
    key_one, key_two = jax.random.split(jax.random.fold_in(key, 17), 2)
    lower = jax.random.randint(key_one, (V,), 0, W // 4 + 1)
    upper = jax.random.randint(key_two, (V,), W - W // 4, W + 1)
    views = jnp.arange(V, dtype=jnp.int32)
    lower = jnp.where(views == 0, 0, lower)
    upper = jnp.where(views == 0, W, upper)
    return jnp.stack([lower, upper], axis=1).astype(jnp.int32)


def draw_final_weight(key, part):
    key_one = jax.random.fold_in(key, 23)
    factor = 4.0
    basic_draw = jnp.clip(jax.random.normal(key_one, (27, CONV), jnp.float32), -4.0, 4.0)
    return (basic_draw * factor / math.sqrt(27.0 * CONV)).astype(jnp.bfloat16)


def bell_draw(own_key, shape, scale, limit, kind=jnp.bfloat16):
    values = jax.random.normal(own_key, shape, jnp.float32) * scale
    return jnp.minimum(jnp.maximum(values, -limit), limit).astype(kind)


def setup_inputs(seed: int = 0) -> dict:
    streams_of = jax.random.split(jax.random.key(seed), 8)
    return {
        "raw_views": draw_raw_views(jax.random.fold_in(streams_of[7], 71), 0),
        "feat_weight": bell_draw(streams_of[1], (9, C, C), (9 * C) ** -0.5, 0.375),
        "shifts": draw_shifts(jax.random.fold_in(streams_of[7], 71), 0),
        "frame_range": draw_frame_range(jax.random.fold_in(streams_of[7], 71), 0),
        "cost_weight": bell_draw(streams_of[4], (27, CONV, C), (27 * C) ** -0.5, 0.21875),
        "mid_weight": bell_draw(streams_of[5], (27, CONV, CONV), (27 * CONV) ** -0.5, 0.4375),
        "final_weight": draw_final_weight(jax.random.fold_in(streams_of[7], 71), 0),
    }


norm_eps = 1e-05

def feature_conv(raw_views, feat_weight):
    row_count = raw_views.shape[2]
    col_total = raw_views.shape[3]
    padded = jnp.pad(raw_views.astype(jnp.float32), ((0, 0), (0, 0), (1, 1), (1, 1)))
    summed = jnp.zeros((raw_views.shape[0], feat_weight.shape[1], row_count, col_total), jnp.float32)
    for kernel_tap in range(9):
        row_off = kernel_tap // 3
        col_off = kernel_tap % 3
        window = padded[:, :, row_off:row_off + row_count, col_off:col_off + col_total]
        summed = summed + jnp.einsum('oi,vihw->vohw', feat_weight[kernel_tap].astype(jnp.float32), window)
    return summed.astype(jnp.bfloat16)

def cost_slice(features, shifts, frame_range, depth_idx):
    depths_all = shifts.shape[1]
    col_total = features.shape[3]
    clipped = jnp.clip(depth_idx, 0, depths_all - 1).astype(jnp.int32)
    view_shift = shifts[:, clipped]
    columns = jnp.arange(col_total, dtype=jnp.int32)
    source = columns[None, :] - view_shift[:, None]
    index_map = jnp.clip(source, 0, col_total - 1).astype(jnp.int32)
    moved = jax.vmap(lambda plane, where_cols: jnp.take(plane, where_cols, axis=2))(features, index_map)
    inside = (source >= frame_range[:, 0:1]) & (source < frame_range[:, 1:2])
    weight_mask = inside.astype(jnp.float32)[:, None, None, :]
    tally = lax.optimization_barrier(jnp.sum(weight_mask, axis=0))
    values = moved.astype(jnp.float32)
    average = lax.optimization_barrier(jnp.sum(weight_mask * values, axis=0)) / tally
    deviation = values - average
    spread = lax.optimization_barrier(jnp.sum(weight_mask * deviation * deviation, axis=0)) / tally
    keep = (depth_idx >= 0) & (depth_idx < depths_all)
    return jnp.where(keep, spread, 0.0).astype(jnp.bfloat16)

def conv_taps(window, weights, amount, row_count, col_count):
    summed = None
    for kernel_tap in range(27):
        depth_off = kernel_tap // 9
        row_off = kernel_tap // 3 % 3
        col_off = kernel_tap % 3
        portion = window[depth_off:depth_off + amount, :, row_off:row_off + row_count, col_off:col_off + col_count]
        term = jnp.einsum('oi,dihw->dohw', weights[kernel_tap].astype(jnp.float32), portion.astype(jnp.float32))
        summed = term if summed is None else summed + term
    return summed

def normalize(values):
    average = lax.optimization_barrier(jnp.mean(values, axis=(0, 2, 3)))
    centered = values - average[None, :, None, None]
    spread = lax.optimization_barrier(jnp.mean(centered * centered, axis=(0, 2, 3)))
    return jnp.maximum(centered * lax.rsqrt(spread + norm_eps)[None, :, None, None], 0.0).astype(jnp.bfloat16)

def conv_full(values, weights):
    depths_all, channels, row_count, col_total = values.shape
    block_len = 8
    padded = jnp.pad(values, ((1, 1), (0, 0), (1, 1), (1, 1)))

    def one_block(index):
        window = lax.dynamic_slice_in_dim(padded, (index * block_len).astype(jnp.int32), block_len + 2, 0)
        return conv_taps(window, weights, block_len, row_count, col_total)
    stacked = lax.map(one_block, jnp.arange(depths_all // block_len, dtype=jnp.int32))
    return stacked.reshape(depths_all, weights.shape[1], row_count, col_total)

def reference(raw_views, feat_weight, shifts, frame_range, cost_weight, mid_weight, final_weight):
    depths_all = shifts.shape[1]
    row_count = raw_views.shape[2]
    col_total = raw_views.shape[3]
    features = feature_conv(raw_views, feat_weight)
    block_len = 8

    def cost_block(index):
        start = (index * block_len).astype(jnp.int32)
        volume = lax.map(lambda depth_step: cost_slice(features, shifts, frame_range, start - 1 + depth_step), jnp.arange(block_len + 2, dtype=jnp.int32))
        framed = jnp.pad(volume, ((0, 0), (0, 0), (1, 1), (1, 1)))
        return conv_taps(framed, cost_weight, block_len, row_count, col_total)
    first_conv = lax.map(cost_block, jnp.arange(depths_all // block_len, dtype=jnp.int32))
    first_conv = first_conv.reshape(depths_all, cost_weight.shape[1], row_count, col_total)
    first_act = normalize(first_conv)
    second_act = normalize(conv_full(first_act, mid_weight))
    score = conv_full(second_act, final_weight[:, None, :])[:, 0]
    peak_value = lax.optimization_barrier(jnp.max(score, axis=0))
    exponent = jnp.exp(score - peak_value[None])
    depth_value = jnp.arange(depths_all, dtype=jnp.float32) / (depths_all - 1)
    return lax.optimization_barrier(jnp.sum(exponent * depth_value[:, None, None], axis=0)) / lax.optimization_barrier(jnp.sum(exponent, axis=0))
```

```python
import jax
import jax.numpy as jnp
from jax import lax
from jax.experimental import pallas as pl
from jax.experimental.pallas import tpu as pltpu
from jax.sharding import PartitionSpec as P

norm_eps = 1e-05

F32 = jnp.float32
BF16 = jnp.bfloat16
I32 = jnp.int32

VIEWS = 8
CHAN = 32
HID = 8
ROWS = 8
DEPTHS = 96
STRIP = 128
OWN = 32
GROUP = 42
HALO = 5
TILES = 32
LEFT = 136
CR = CHAN * ROWS
HR = HID * ROWS
DEVICES = 256
COUNT = DEPTHS * ROWS * OWN

VMEM = pl.BlockSpec(memory_space=pltpu.VMEM)
SMEM = pl.BlockSpec(memory_space=pltpu.SMEM)
PARAMS = pltpu.CompilerParams(vmem_limit_bytes=48 * 1024 * 1024)


def iota(shape, axis):
    return lax.broadcasted_iota(I32, shape, axis)


def mm(a, b):
    return jnp.dot(a, b, preferred_element_type=F32)


def spread_rows(count):
    return ((iota((8 * count, count), 0) >> 3) == iota((8 * count, count), 1)).astype(F32).astype(BF16)


def spread_cols(count):
    return (iota((count, 8 * count), 0) == (iota((count, 8 * count), 1) >> 3)).astype(F32).astype(BF16)


def banded(taps, left, right):
    total = None
    for b, w in enumerate(taps):
        t = w if left is None else mm(left, w).astype(BF16)
        u = mm(t, right)
        rows, cols = u.shape
        band = ((iota((rows, cols), 1) & 7) - (iota((rows, cols), 0) & 7)) == (b - 1)
        u = jnp.where(band, u, 0.0)
        total = u if total is None else total + u
    return total


def weights_kernel(fw, cw, mw, lw, wf, w1, w2, w3):
    ro32, ro8 = spread_rows(CHAN), spread_rows(HID)
    ci32, ci8 = spread_cols(CHAN), spread_cols(HID)
    for b in range(3):
        wf[b * CR : (b + 1) * CR, :] = banded([fw[3 * a + b] for a in range(3)], ro32, ci32).astype(BF16)
    for a in range(3):
        for e in range(3):
            taps = [9 * a + 3 * b + e for b in range(3)]
            w1[e * HR : (e + 1) * HR, a * CR : (a + 1) * CR] = banded(
                [cw[t] for t in taps], ro8, ci32
            ).astype(BF16)
    second, last = [], []
    for e in range(3):
        row2, row3 = [], []
        for a in range(3):
            taps = [9 * a + 3 * b + e for b in range(3)]
            row2.append(banded([mw[t] for t in taps], ro8, ci8))
            row3.append(
                banded([jnp.broadcast_to(lw[t], (ROWS, HID)).astype(BF16) for t in taps], None, ci8)
            )
        second.append(jnp.concatenate(row2, axis=1))
        last.append(jnp.concatenate(row3, axis=1))
    w2[...] = jnp.concatenate(second, axis=0).astype(BF16)
    w3[...] = jnp.concatenate(last, axis=0).astype(BF16)


def make_weights(feat_weight, cost_weight, mid_weight, final_weight):
    return pl.pallas_call(
        weights_kernel,
        out_shape=(
            jax.ShapeDtypeStruct((3 * CR, CR), BF16),
            jax.ShapeDtypeStruct((3 * HR, 3 * CR), BF16),
            jax.ShapeDtypeStruct((3 * HR, 3 * HR), BF16),
            jax.ShapeDtypeStruct((3 * ROWS, 3 * HR), BF16),
        ),
        in_specs=[VMEM] * 4,
        out_specs=(VMEM,) * 4,
        compiler_params=PARAMS,
        cost_estimate=pl.CostEstimate(flops=2_000_000_000, bytes_accessed=1_000_000, transcendentals=0),
        name="banded_weights",
    )(feat_weight, cost_weight, mid_weight, final_weight.astype(F32).reshape(27, 1, HID))


def features_kernel(pos, s2, s1, s0, sp, wf, *outs):
    depth = pos[0]
    for u in range(2):
        x = jnp.concatenate([s2[u], s1[u], s0[u], sp[u]], axis=1)
        y = mm(wf[...], x)
        f = (
            y[CR : 2 * CR]
            + pltpu.roll(y[:CR], 1, axis=1)
            + pltpu.roll(y[2 * CR :], 4 * STRIP - 1, axis=1)
        )
        f = f.astype(BF16).astype(F32)
        for k in range(4):
            target = depth ^ k
            start = OWN * target + 2 * STRIP - LEFT
            outs[k][u] = pltpu.roll(f, 4 * STRIP - start, axis=1)[:, : 2 * STRIP].astype(BF16)


def make_features(pos, strips, wf):
    return pl.pallas_call(
        features_kernel,
        out_shape=tuple(jax.ShapeDtypeStruct((2, CR, 2 * STRIP), BF16) for _ in range(4)),
        in_specs=[SMEM] + [VMEM] * 5,
        out_specs=(VMEM,) * 4,
        compiler_params=PARAMS,
        name="features",
    )(pos, *strips, wf)


def lane_places(width):
    lane = iota((1, width), 1) & (STRIP - 1)
    group = (lane >= GROUP).astype(I32) + (lane >= 2 * GROUP).astype(I32)
    return lane, group, lane - GROUP * group - HALO


def wrap_tiles(ref, size):
    lane = iota((1, STRIP), 1)
    last = ref[TILES * size : (TILES + 1) * size, :].astype(F32)
    first = ref[size : 2 * size, :].astype(F32)
    before = jnp.where(lane >= GROUP, pltpu.roll(last, GROUP, axis=1), 0.0)
    after = jnp.where(lane < 2 * GROUP, pltpu.roll(first, STRIP - GROUP, axis=1), 0.0)
    ref[0:size, :] = before.astype(BF16)
    ref[(TILES + 1) * size : (TILES + 2) * size, :] = after.astype(BF16)


def own_mask():
    lane, _, col = lane_places(STRIP)
    return ((col >= 0) & (col < OWN)).astype(F32)


def total_of(x):
    return jnp.sum(jnp.sum(x, axis=0, keepdims=True), axis=1, keepdims=True)


def conv_and_stats(w, ref, size, out, stats):
    mask = own_mask()

    def one(k, acc):
        rows = ref[pl.ds(pl.multiple_of(k * size, size), 3 * size), :]
        z = mm(w[...], rows)
        y = z[HR : 2 * HR] + pltpu.roll(z[:HR], 1, axis=1) + pltpu.roll(z[2 * HR :], STRIP - 1, axis=1)
        out[pl.ds(pl.multiple_of(k * HR, HR), HR), :] = y
        return acc + y

    acc = lax.fori_loop(0, TILES, one, jnp.zeros((HR, STRIP), F32), unroll=4) * mask
    means = [total_of(acc[ROWS * o : ROWS * (o + 1)]) * (1.0 / COUNT) for o in range(HID)]
    mean = jnp.concatenate([jnp.broadcast_to(m, (ROWS, STRIP)) for m in means], axis=0)

    def two(k, acc):
        dev = (out[pl.ds(pl.multiple_of(k * HR, HR), HR), :] - mean) * mask
        return acc + dev * dev

    acc = lax.fori_loop(0, TILES, two, jnp.zeros((HR, STRIP), F32), unroll=4)
    lane = iota((1, STRIP), 1)
    row = jnp.zeros((1, STRIP), F32)
    for o in range(HID):
        row = jnp.where(lane == o, means[o], row)
        row = jnp.where(lane == HID + o, total_of(acc[ROWS * o : ROWS * (o + 1)]), row)
    stats[...] = jnp.broadcast_to(row, (DEVICES, STRIP))


def normalized(pos, stats, values, act):
    lane = iota((1, STRIP), 1)
    rows = stats[...]
    center = jnp.sum(rows, axis=0, keepdims=True) * (1.0 / DEVICES)
    dev = rows - center
    between = jnp.sum(dev * dev, axis=0, keepdims=True)

    def pick(row, at):
        return jnp.sum(jnp.where(lane == at, row, 0.0), axis=1, keepdims=True)

    means, scales = [], []
    for o in range(HID):
        spread = pick(center, HID + o) * (1.0 / COUNT) + pick(between, o) * (1.0 / DEVICES)
        means.append(jnp.broadcast_to(pick(center, o), (ROWS, STRIP)))
        scales.append(jnp.broadcast_to(lax.rsqrt(spread + norm_eps), (ROWS, STRIP)))
    mean = jnp.concatenate(means, axis=0)
    scale = jnp.concatenate(scales, axis=0)
    _, _, col = lane_places(STRIP)
    col = col + (STRIP * pos[1] + OWN * pos[0])
    inside = (col >= 0) & (col < STRIP * pos[2])

    def one(k, carry):
        x = values[pl.ds(pl.multiple_of(k * HR, HR), HR), :]
        y = jnp.where(inside, jnp.maximum((x - mean) * scale, 0.0), 0.0)
        act[pl.ds(pl.multiple_of((k + 1) * HR, HR), HR), :] = y.astype(BF16)
        return carry

    lax.fori_loop(0, TILES, one, 0, unroll=4)
    wrap_tiles(act, HR)


def volume_kernel(pos, shifts, frame, f0, f1, f2, f3, w1, out, stats, moved, vol):
    depth = pos[0]
    base = STRIP * pos[1] + OWN * depth
    wide = 2 * STRIP
    _, group, col = lane_places(wide)
    half = iota((1, wide), 1) >= STRIP
    glob = base + col
    valid = (glob >= 0) & (glob < STRIP * pos[2])
    places = iota((wide, wide), 0)
    sources = (f0, f1, f2, f3)

    def pair(kk, carry):
        masks = []
        for n in range(VIEWS):
            v = 2 * (depth ^ (n // 2)) + n % 2
            at = [[shifts[v, TILES * j + 2 * kk + s] for j in range(3)] for s in range(2)]
            one, two = (
                jnp.where(group == 0, t[0], jnp.where(group == 1, t[1], t[2])) for t in at
            )
            shift = jnp.where(half, two, one)
            source = glob - shift
            inside = (source >= frame[v, 0]) & (source < frame[v, 1])
            index = jnp.where(inside, col - shift + LEFT, -1)
            hot = jnp.where(places == index, 1.0, 0.0).astype(BF16)
            moved[n] = mm(sources[n // 2][n % 2], hot)
            masks.append(inside.astype(F32))
        tally = masks[0]
        for m in masks[1:]:
            tally = tally + m
        inverse = 1.0 / tally
        for r in range(0, CR, 16):
            parts = [moved[n, r : r + 16, :] for n in range(VIEWS)]
            total = parts[0]
            for p in parts[1:]:
                total = total + p
            average = total * inverse
            spread = None
            for p, m in zip(parts, masks):
                dev = (p - average) * m
                spread = dev * dev if spread is None else spread + dev * dev
            value = jnp.where(valid, spread * inverse, 0.0).astype(BF16)
            for s in range(2):
                row = pl.multiple_of((2 * kk + s + 1) * CR + r, 16)
                vol[pl.ds(row, 16), :] = value[:, s * STRIP : (s + 1) * STRIP]
        return carry

    lax.fori_loop(0, TILES // 2, pair, 0)
    wrap_tiles(vol, CR)
    conv_and_stats(w1, vol, CR, out, stats)


def cost_and_conv(pos, shifts, frame, feats, w1):
    return pl.pallas_call(
        volume_kernel,
        out_shape=(
            jax.ShapeDtypeStruct((TILES * HR, STRIP), F32),
            jax.ShapeDtypeStruct((DEVICES, STRIP), F32),
        ),
        in_specs=[SMEM] * 3 + [VMEM] * 5,
        out_specs=(VMEM,) * 2,
        scratch_shapes=[
            pltpu.VMEM((VIEWS, CR, 2 * STRIP), F32),
            pltpu.VMEM(((TILES + 2) * CR, STRIP), BF16),
        ],
        compiler_params=PARAMS,
        name="cost_volume",
    )(pos, shifts, frame, *feats, w1)


def middle_kernel(pos, stats_in, values, w2, out, stats, act):
    normalized(pos, stats_in, values, act)
    conv_and_stats(w2, act, HR, out, stats)


def second_conv(pos, stats, values, w2):
    return pl.pallas_call(
        middle_kernel,
        out_shape=(
            jax.ShapeDtypeStruct((TILES * HR, STRIP), F32),
            jax.ShapeDtypeStruct((DEVICES, STRIP), F32),
        ),
        in_specs=[SMEM] + [VMEM] * 3,
        out_specs=(VMEM,) * 2,
        scratch_shapes=[pltpu.VMEM(((TILES + 2) * HR, STRIP), BF16)],
        compiler_params=PARAMS,
        name="second_conv",
    )(pos, stats, values, w2)


def last_kernel(pos, stats_in, values, w3, out, act, score):
    normalized(pos, stats_in, values, act)

    def one(k, peak):
        z = mm(w3[...], act[pl.ds(pl.multiple_of(k * HR, HR), 3 * HR), :])
        y = (
            z[ROWS : 2 * ROWS]
            + pltpu.roll(z[:ROWS], 1, axis=1)
            + pltpu.roll(z[2 * ROWS :], STRIP - 1, axis=1)
        )
        score[k] = y
        return jnp.maximum(peak, y)

    peak = lax.fori_loop(0, TILES, one, jnp.full((ROWS, STRIP), -jnp.inf, F32), unroll=4)
    _, group, _ = lane_places(STRIP)

    def two(k, sums):
        e = jnp.exp(score[k] - peak)
        value = (TILES * group + k).astype(F32) / (DEPTHS - 1)
        return sums[0] + e, sums[1] + e * value

    zero = jnp.zeros((ROWS, STRIP), F32)
    total, weighted = lax.fori_loop(0, TILES, two, (zero, zero), unroll=4)

    def turned(x):
        return [x] + [pltpu.roll(x, STRIP - j * GROUP, axis=1) for j in (1, 2)]

    peaks, totals, weights = turned(peak), turned(total), turned(weighted)
    top = jnp.maximum(jnp.maximum(peaks[0], peaks[1]), peaks[2])
    scales = [jnp.exp(p - top) for p in peaks]
    whole = sum(t * s for t, s in zip(totals, scales))
    mean = sum(t * s for t, s in zip(weights, scales)) / whole
    first = OWN * pos[0]
    lane = iota((1, STRIP), 1)
    moved = pltpu.roll(mean, (first + STRIP - HALO) & (STRIP - 1), axis=1)
    out[...] = jnp.where((lane >= first) & (lane < first + OWN), moved, 0.0)


def final_estimate(pos, stats, values, w3):
    return pl.pallas_call(
        last_kernel,
        out_shape=jax.ShapeDtypeStruct((ROWS, STRIP), F32),
        in_specs=[SMEM] + [VMEM] * 3,
        out_specs=VMEM,
        scratch_shapes=[
            pltpu.VMEM(((TILES + 2) * HR, STRIP), BF16),
            pltpu.VMEM((TILES, ROWS, STRIP), F32),
        ],
        compiler_params=PARAMS,
        name="final_estimate",
    )(pos, stats, values, w3)


def beside(x, by):
    peers = lax.axis_size("col")
    return lax.ppermute(x, "col", [(i, i + by) for i in range(peers) if 0 <= i + by < peers])


def everyones(stats):
    return lax.all_to_all(stats, ("depth", "col"), 0, 0, tiled=True)


def local(raw_views, feat_weight, shifts, frame_range, cost_weight, mid_weight, final_weight):
    pos = jnp.stack([lax.axis_index("depth"), lax.axis_index("col"), jnp.int32(lax.axis_size("col"))])
    pos = pos.astype(I32)
    own = raw_views.reshape(2, CR, STRIP)
    with jax.named_scope("strips"):
        strips = (beside(own, 2), beside(own, 1), own, beside(own, -1))
    wf, w1, w2, w3 = make_weights(feat_weight, cost_weight, mid_weight, final_weight)
    windows = make_features(pos, strips, wf)
    with jax.named_scope("views"):
        feats = [windows[0]] + [
            lax.ppermute(windows[k], "depth", [(i, i ^ k) for i in range(4)]) for k in (1, 2, 3)
        ]
    first, stats = cost_and_conv(pos, shifts, frame_range, feats, w1)
    second, stats = second_conv(pos, everyones(stats), first, w2)
    part = final_estimate(pos, everyones(stats), second, w3)
    return lax.psum(part, "depth")


def solution(mesh):
    in_specs = (P("depth", None, None, "col"), P(), P(), P(), P(), P(), P())
    out_specs = P(None, "col")
    return jax.shard_map(local, mesh=mesh, in_specs=in_specs, out_specs=out_specs, check_vma=False)
```

```python
import jax
import jax.numpy as jnp
from jax import lax
from jax.experimental import pallas as pl
from jax.experimental.pallas import tpu as pltpu
from jax.sharding import PartitionSpec as P

norm_eps = 1e-05

F32 = jnp.float32
BF16 = jnp.bfloat16
I32 = jnp.int32

VIEWS = 8
CHAN = 32
HID = 8
ROWS = 8
DEPTHS = 96
STRIP = 128
OWN = 32
GROUP = 42
HALO = 5
TILES = 32
LEFT = 136
BASE = 176
CR = CHAN * ROWS
HR = HID * ROWS
DEVICES = 256
COUNT = DEPTHS * ROWS * OWN

VMEM = pl.BlockSpec(memory_space=pltpu.VMEM)
SMEM = pl.BlockSpec(memory_space=pltpu.SMEM)
PARAMS = pltpu.CompilerParams(vmem_limit_bytes=48 * 1024 * 1024)


def iota(shape, axis):
    return lax.broadcasted_iota(I32, shape, axis)


def mm(a, b):
    return jnp.dot(a, b, preferred_element_type=F32)


def spread_rows(count):
    return ((iota((8 * count, count), 0) >> 3) == iota((8 * count, count), 1)).astype(F32).astype(BF16)


def spread_cols(count):
    return (iota((count, 8 * count), 0) == (iota((count, 8 * count), 1) >> 3)).astype(F32).astype(BF16)


def banded(taps, left, right):
    total = None
    for b, w in enumerate(taps):
        t = w if left is None else mm(left, w).astype(BF16)
        u = mm(t, right)
        rows, cols = u.shape
        band = ((iota((rows, cols), 1) & 7) - (iota((rows, cols), 0) & 7)) == (b - 1)
        u = jnp.where(band, u, 0.0)
        total = u if total is None else total + u
    return total


def weights_kernel(fw, cw, mw, lw, wf, w1, w2, w3):
    ro32, ro8 = spread_rows(CHAN), spread_rows(HID)
    ci32, ci8 = spread_cols(CHAN), spread_cols(HID)
    for b in range(3):
        wf[b * CR : (b + 1) * CR, :] = banded([fw[3 * a + b] for a in range(3)], ro32, ci32).astype(BF16)
    for a in range(3):
        for e in range(3):
            taps = [9 * a + 3 * b + e for b in range(3)]
            w1[e * HR : (e + 1) * HR, a * CR : (a + 1) * CR] = banded(
                [cw[t] for t in taps], ro8, ci32
            ).astype(BF16)
    second, last = [], []
    for e in range(3):
        row2, row3 = [], []
        for a in range(3):
            taps = [9 * a + 3 * b + e for b in range(3)]
            row2.append(banded([mw[t] for t in taps], ro8, ci8))
            row3.append(
                banded([jnp.broadcast_to(lw[t], (ROWS, HID)).astype(BF16) for t in taps], None, ci8)
            )
        second.append(jnp.concatenate(row2, axis=1))
        last.append(jnp.concatenate(row3, axis=1))
    w2[...] = jnp.concatenate(second, axis=0).astype(BF16)
    w3[...] = jnp.concatenate(last, axis=0).astype(BF16)


def make_weights(feat_weight, cost_weight, mid_weight, final_weight):
    return pl.pallas_call(
        weights_kernel,
        out_shape=(
            jax.ShapeDtypeStruct((3 * CR, CR), BF16),
            jax.ShapeDtypeStruct((3 * HR, 3 * CR), BF16),
            jax.ShapeDtypeStruct((3 * HR, 3 * HR), BF16),
            jax.ShapeDtypeStruct((3 * ROWS, 3 * HR), BF16),
        ),
        in_specs=[VMEM] * 4,
        out_specs=(VMEM,) * 4,
        compiler_params=PARAMS,
        cost_estimate=pl.CostEstimate(flops=2_000_000_000, bytes_accessed=1_000_000, transcendentals=0),
        name="banded_weights",
    )(feat_weight, cost_weight, mid_weight, final_weight.astype(F32).reshape(27, 1, HID))


def features_kernel(pos, s2, s1, s0, sp, wf, *outs):
    depth = pos[0]
    for u in range(2):
        x = jnp.concatenate([s2[u], s1[u], s0[u], sp[u]], axis=1)
        y = mm(wf[...], x)
        f = (
            y[CR : 2 * CR]
            + pltpu.roll(y[:CR], 1, axis=1)
            + pltpu.roll(y[2 * CR :], 4 * STRIP - 1, axis=1)
        )
        f = f.astype(BF16).astype(F32)
        for k in range(4):
            target = depth ^ k
            start = OWN * target + 2 * STRIP - LEFT
            outs[k][u] = pltpu.roll(f, 4 * STRIP - start, axis=1)[:, : 2 * STRIP].astype(BF16)


def make_features(pos, strips, wf):
    return pl.pallas_call(
        features_kernel,
        out_shape=tuple(jax.ShapeDtypeStruct((2, CR, 2 * STRIP), BF16) for _ in range(4)),
        in_specs=[SMEM] + [VMEM] * 5,
        out_specs=(VMEM,) * 4,
        compiler_params=PARAMS,
        name="features",
    )(pos, *strips, wf)


def lane_places(width):
    lane = iota((1, width), 1) & (STRIP - 1)
    group = (lane >= GROUP).astype(I32) + (lane >= 2 * GROUP).astype(I32)
    return lane, group, lane - GROUP * group - HALO


def wrap_tiles(ref, size):
    lane = iota((1, STRIP), 1)
    last = ref[TILES * size : (TILES + 1) * size, :].astype(F32)
    first = ref[size : 2 * size, :].astype(F32)
    before = jnp.where(lane >= GROUP, pltpu.roll(last, GROUP, axis=1), 0.0)
    after = jnp.where(lane < 2 * GROUP, pltpu.roll(first, STRIP - GROUP, axis=1), 0.0)
    ref[0:size, :] = before.astype(BF16)
    ref[(TILES + 1) * size : (TILES + 2) * size, :] = after.astype(BF16)


def own_mask():
    lane, _, col = lane_places(STRIP)
    return ((col >= 0) & (col < OWN)).astype(F32)


def total_of(x):
    return jnp.sum(jnp.sum(x, axis=0, keepdims=True), axis=1, keepdims=True)


def conv_and_stats(w, ref, size, out, stats):
    mask = own_mask()

    def one(k, acc):
        rows = ref[pl.ds(pl.multiple_of(k * size, size), 3 * size), :]
        z = mm(w[...], rows)
        y = z[HR : 2 * HR] + pltpu.roll(z[:HR], 1, axis=1) + pltpu.roll(z[2 * HR :], STRIP - 1, axis=1)
        out[pl.ds(pl.multiple_of(k * HR, HR), HR), :] = y
        return acc + y

    acc = lax.fori_loop(0, TILES, one, jnp.zeros((HR, STRIP), F32), unroll=4) * mask
    means = [total_of(acc[ROWS * o : ROWS * (o + 1)]) * (1.0 / COUNT) for o in range(HID)]
    mean = jnp.concatenate([jnp.broadcast_to(m, (ROWS, STRIP)) for m in means], axis=0)

    def two(k, acc):
        dev = (out[pl.ds(pl.multiple_of(k * HR, HR), HR), :] - mean) * mask
        return acc + dev * dev

    acc = lax.fori_loop(0, TILES, two, jnp.zeros((HR, STRIP), F32), unroll=4)
    lane = iota((1, STRIP), 1)
    row = jnp.zeros((1, STRIP), F32)
    for o in range(HID):
        row = jnp.where(lane == o, means[o], row)
        row = jnp.where(lane == HID + o, total_of(acc[ROWS * o : ROWS * (o + 1)]), row)
    stats[...] = jnp.broadcast_to(row, (DEVICES, STRIP))


def normalized(pos, stats, values, act):
    lane = iota((1, STRIP), 1)
    rows = stats[...]
    center = jnp.sum(rows, axis=0, keepdims=True) * (1.0 / DEVICES)
    dev = rows - center
    between = jnp.sum(dev * dev, axis=0, keepdims=True)

    def pick(row, at):
        return jnp.sum(jnp.where(lane == at, row, 0.0), axis=1, keepdims=True)

    means, scales = [], []
    for o in range(HID):
        spread = pick(center, HID + o) * (1.0 / COUNT) + pick(between, o) * (1.0 / DEVICES)
        means.append(jnp.broadcast_to(pick(center, o), (ROWS, STRIP)))
        scales.append(jnp.broadcast_to(lax.rsqrt(spread + norm_eps), (ROWS, STRIP)))
    mean = jnp.concatenate(means, axis=0)
    scale = jnp.concatenate(scales, axis=0)
    _, _, col = lane_places(STRIP)
    col = col + (STRIP * pos[1] + OWN * pos[0])
    inside = (col >= 0) & (col < STRIP * pos[2])

    def one(k, carry):
        x = values[pl.ds(pl.multiple_of(k * HR, HR), HR), :]
        y = jnp.where(inside, jnp.maximum((x - mean) * scale, 0.0), 0.0)
        act[pl.ds(pl.multiple_of((k + 1) * HR, HR), HR), :] = y.astype(BF16)
        return carry

    lax.fori_loop(0, TILES, one, 0, unroll=4)
    wrap_tiles(act, HR)


def volume_kernel(pos, shifts, frame, f0, f1, f2, f3, w1, out, stats, feats, even, odd, vol):
    depth = pos[0]
    base = STRIP * pos[1] + OWN * depth
    wide = 2 * STRIP
    lane = iota((1, wide), 1)
    sources = (f0, f1, f2, f3)
    for k in range(4):
        for u in range(2):
            feats[2 * (depth ^ k) + u] = sources[k][u]
    zero_view = pltpu.roll(feats[0].astype(F32), BASE - (LEFT - HALO), axis=1)
    own_lanes = (lane >= BASE) & (lane < BASE + GROUP)
    for v in range(1, VIEWS):
        feats[v] = jnp.where(own_lanes, zero_view, feats[v].astype(F32)).astype(BF16)

    _, group, col = lane_places(wide)
    half = lane >= STRIP
    glob = base + col
    valid = (glob >= 0) & (glob < STRIP * pos[2])
    places = iota((BASE, wide), 0)
    below = jnp.where(iota((wide - BASE, wide), 0) == col + HALO, -1.0, 0.0)

    def move(kk, moved):
        tally = jnp.ones((1, wide), F32)
        for v in range(1, VIEWS):
            at = [[shifts[v, TILES * j + 2 * kk + s] for j in range(3)] for s in range(2)]
            one, two = (
                jnp.where(group == 0, t[0], jnp.where(group == 1, t[1], t[2])) for t in at
            )
            shift = jnp.where(half, two, one)
            source = glob - shift
            inside = (source >= frame[v, 0]) & (source < frame[v, 1])
            index = jnp.where(inside, col - shift + LEFT, -1)
            hot = jnp.where(places == index, 1.0, 0.0).astype(BF16)
            mask = inside.astype(F32)
            hot = jnp.concatenate([hot, (below * mask).astype(BF16)], axis=0)
            moved[v - 1] = mm(feats[v], hot)
            tally = tally + mask
        return 1.0 / tally

    def spread(kk, moved, inverse):
        for r in range(0, CR, 16):
            total = squares = None
            for v in range(VIEWS - 1):
                p = moved[v, r : r + 16, :]
                total = p if total is None else total + p
                squares = p * p if squares is None else squares + p * p
            average = total * inverse
            value = jnp.where(valid, squares * inverse - average * average, 0.0)
            value = jnp.maximum(value, 0.0).astype(BF16)
            for s in range(2):
                row = pl.multiple_of((2 * kk + s + 1) * CR + r, 16)
                vol[pl.ds(row, 16), :] = value[:, s * STRIP : (s + 1) * STRIP]

    def step(t, inverse):
        spread(2 * t, even, inverse)
        later = move(2 * t + 1, odd)
        spread(2 * t + 1, odd, later)
        return move(jnp.minimum(2 * t + 2, TILES // 2 - 1), even)

    lax.fori_loop(0, TILES // 4, step, move(0, even))
    wrap_tiles(vol, CR)
    conv_and_stats(w1, vol, CR, out, stats)


def cost_and_conv(pos, shifts, frame, feats, w1):
    return pl.pallas_call(
        volume_kernel,
        out_shape=(
            jax.ShapeDtypeStruct((TILES * HR, STRIP), F32),
            jax.ShapeDtypeStruct((DEVICES, STRIP), F32),
        ),
        in_specs=[SMEM] * 3 + [VMEM] * 5,
        out_specs=(VMEM,) * 2,
        scratch_shapes=[
            pltpu.VMEM((VIEWS, CR, 2 * STRIP), BF16),
            pltpu.VMEM((VIEWS - 1, CR, 2 * STRIP), F32),
            pltpu.VMEM((VIEWS - 1, CR, 2 * STRIP), F32),
            pltpu.VMEM(((TILES + 2) * CR, STRIP), BF16),
        ],
        compiler_params=PARAMS,
        name="cost_volume",
    )(pos, shifts, frame, *feats, w1)


def middle_kernel(pos, stats_in, values, w2, out, stats, act):
    normalized(pos, stats_in, values, act)
    conv_and_stats(w2, act, HR, out, stats)


def second_conv(pos, stats, values, w2):
    return pl.pallas_call(
        middle_kernel,
        out_shape=(
            jax.ShapeDtypeStruct((TILES * HR, STRIP), F32),
            jax.ShapeDtypeStruct((DEVICES, STRIP), F32),
        ),
        in_specs=[SMEM] + [VMEM] * 3,
        out_specs=(VMEM,) * 2,
        scratch_shapes=[pltpu.VMEM(((TILES + 2) * HR, STRIP), BF16)],
        compiler_params=PARAMS,
        name="second_conv",
    )(pos, stats, values, w2)


def last_kernel(pos, stats_in, values, w3, out, act, score):
    normalized(pos, stats_in, values, act)

    def one(k, peak):
        z = mm(w3[...], act[pl.ds(pl.multiple_of(k * HR, HR), 3 * HR), :])
        y = (
            z[ROWS : 2 * ROWS]
            + pltpu.roll(z[:ROWS], 1, axis=1)
            + pltpu.roll(z[2 * ROWS :], STRIP - 1, axis=1)
        )
        score[k] = y
        return jnp.maximum(peak, y)

    peak = lax.fori_loop(0, TILES, one, jnp.full((ROWS, STRIP), -jnp.inf, F32), unroll=4)
    _, group, _ = lane_places(STRIP)

    def two(k, sums):
        e = jnp.exp(score[k] - peak)
        value = (TILES * group + k).astype(F32) / (DEPTHS - 1)
        return sums[0] + e, sums[1] + e * value

    zero = jnp.zeros((ROWS, STRIP), F32)
    total, weighted = lax.fori_loop(0, TILES, two, (zero, zero), unroll=4)

    def turned(x):
        return [x] + [pltpu.roll(x, STRIP - j * GROUP, axis=1) for j in (1, 2)]

    peaks, totals, weights = turned(peak), turned(total), turned(weighted)
    top = jnp.maximum(jnp.maximum(peaks[0], peaks[1]), peaks[2])
    scales = [jnp.exp(p - top) for p in peaks]
    whole = sum(t * s for t, s in zip(totals, scales))
    mean = sum(t * s for t, s in zip(weights, scales)) / whole
    first = OWN * pos[0]
    lane = iota((1, STRIP), 1)
    moved = pltpu.roll(mean, (first + STRIP - HALO) & (STRIP - 1), axis=1)
    out[...] = jnp.where((lane >= first) & (lane < first + OWN), moved, 0.0)


def final_estimate(pos, stats, values, w3):
    return pl.pallas_call(
        last_kernel,
        out_shape=jax.ShapeDtypeStruct((ROWS, STRIP), F32),
        in_specs=[SMEM] + [VMEM] * 3,
        out_specs=VMEM,
        scratch_shapes=[
            pltpu.VMEM(((TILES + 2) * HR, STRIP), BF16),
            pltpu.VMEM((TILES, ROWS, STRIP), F32),
        ],
        compiler_params=PARAMS,
        name="final_estimate",
    )(pos, stats, values, w3)


def beside(x, by):
    peers = lax.axis_size("col")
    return lax.ppermute(x, "col", [(i, i + by) for i in range(peers) if 0 <= i + by < peers])


def everyones(stats):
    return lax.all_to_all(stats, ("depth", "col"), 0, 0, tiled=True)


def local(raw_views, feat_weight, shifts, frame_range, cost_weight, mid_weight, final_weight):
    pos = jnp.stack([lax.axis_index("depth"), lax.axis_index("col"), jnp.int32(lax.axis_size("col"))])
    pos = pos.astype(I32)
    own = raw_views.reshape(2, CR, STRIP)
    with jax.named_scope("strips"):
        strips = (beside(own, 2), beside(own, 1), own, beside(own, -1))
    wf, w1, w2, w3 = make_weights(feat_weight, cost_weight, mid_weight, final_weight)
    windows = make_features(pos, strips, wf)
    with jax.named_scope("views"):
        feats = [windows[0]] + [
            lax.ppermute(windows[k], "depth", [(i, i ^ k) for i in range(4)]) for k in (1, 2, 3)
        ]
    first, stats = cost_and_conv(pos, shifts, frame_range, feats, w1)
    second, stats = second_conv(pos, everyones(stats), first, w2)
    part = final_estimate(pos, everyones(stats), second, w3)
    with jax.named_scope("columns"):
        others = [lax.ppermute(part, "depth", [(i, i ^ k) for i in range(4)]) for k in (1, 2, 3)]
        return part + others[0] + others[1] + others[2]


def solution(mesh):
    in_specs = (P("depth", None, None, "col"), P(), P(), P(), P(), P(), P())
    out_specs = P(None, "col")
    return jax.shard_map(local, mesh=mesh, in_specs=in_specs, out_specs=out_specs, check_vma=False)
```

```python
import jax
import jax.numpy as jnp
from jax import lax
from jax.experimental import pallas as pl
from jax.experimental.pallas import tpu as pltpu
from jax.sharding import PartitionSpec as P

norm_eps = 1e-05

F32 = jnp.float32
BF16 = jnp.bfloat16
I32 = jnp.int32

VIEWS = 8
CHAN = 32
HID = 8
ROWS = 8
DEPTHS = 96
STRIP = 128
OWN = 32
GROUP = 42
HALO = 5
TILES = 32
LEFT = 136
EDGE = 8
BASE = 176
CR = CHAN * ROWS
HR = HID * ROWS
DEVICES = 256
COUNT = DEPTHS * ROWS * OWN

VMEM = pl.BlockSpec(memory_space=pltpu.VMEM)
SMEM = pl.BlockSpec(memory_space=pltpu.SMEM)
PARAMS = pltpu.CompilerParams(vmem_limit_bytes=48 * 1024 * 1024)


def iota(shape, axis):
    return lax.broadcasted_iota(I32, shape, axis)


def mm(a, b):
    return jnp.dot(a, b, preferred_element_type=F32)


def spread_rows(count):
    return ((iota((8 * count, count), 0) >> 3) == iota((8 * count, count), 1)).astype(F32).astype(BF16)


def spread_cols(count):
    return (iota((count, 8 * count), 0) == (iota((count, 8 * count), 1) >> 3)).astype(F32).astype(BF16)


def banded(taps, left, right):
    total = None
    for b, w in enumerate(taps):
        t = w if left is None else mm(left, w).astype(BF16)
        u = mm(t, right)
        rows, cols = u.shape
        band = ((iota((rows, cols), 1) & 7) - (iota((rows, cols), 0) & 7)) == (b - 1)
        u = jnp.where(band, u, 0.0)
        total = u if total is None else total + u
    return total


def weights_kernel(fw, cw, mw, lw, wf, w1, w2, w3):
    ro32, ro8 = spread_rows(CHAN), spread_rows(HID)
    ci32, ci8 = spread_cols(CHAN), spread_cols(HID)
    for b in range(3):
        wf[b * CR : (b + 1) * CR, :] = banded([fw[3 * a + b] for a in range(3)], ro32, ci32).astype(BF16)
    for a in range(3):
        for e in range(3):
            taps = [9 * a + 3 * b + e for b in range(3)]
            w1[e * HR : (e + 1) * HR, a * CR : (a + 1) * CR] = banded(
                [cw[t] for t in taps], ro8, ci32
            ).astype(BF16)
    second, last = [], []
    for e in range(3):
        row2, row3 = [], []
        for a in range(3):
            taps = [9 * a + 3 * b + e for b in range(3)]
            row2.append(banded([mw[t] for t in taps], ro8, ci8))
            row3.append(
                banded([jnp.broadcast_to(lw[t], (ROWS, HID)).astype(BF16) for t in taps], None, ci8)
            )
        second.append(jnp.concatenate(row2, axis=1))
        last.append(jnp.concatenate(row3, axis=1))
    w2[...] = jnp.concatenate(second, axis=0).astype(BF16)
    w3[...] = jnp.concatenate(last, axis=0).astype(BF16)


def make_weights(feat_weight, cost_weight, mid_weight, final_weight):
    return pl.pallas_call(
        weights_kernel,
        out_shape=(
            jax.ShapeDtypeStruct((3 * CR, CR), BF16),
            jax.ShapeDtypeStruct((3 * HR, 3 * CR), BF16),
            jax.ShapeDtypeStruct((3 * HR, 3 * HR), BF16),
            jax.ShapeDtypeStruct((3 * ROWS, 3 * HR), BF16),
        ),
        in_specs=[VMEM] * 4,
        out_specs=(VMEM,) * 4,
        compiler_params=PARAMS,
        cost_estimate=pl.CostEstimate(flops=2_000_000_000, bytes_accessed=1_000_000, transcendentals=0),
        name="banded_weights",
    )(feat_weight, cost_weight, mid_weight, final_weight.astype(F32).reshape(27, 1, HID))


def views_kernel(pos, r0, r1, r2, r3, every, edge):
    depth = pos[0]
    for k, r in enumerate((r0, r1, r2, r3)):
        for u in range(2):
            every[2 * (depth ^ k) + u] = r[u]
    lane = iota((1, STRIP), 1)
    turn = jnp.where(depth == 0, EDGE, 0)
    packed = jnp.zeros((CR, STRIP), F32)
    for v in range(VIEWS):
        x = pltpu.roll(every[v].astype(F32), turn + EDGE * v, axis=1)
        packed = jnp.where((lane >> 3) == v, x, packed)
    edge[...] = packed.astype(BF16)


def all_views(pos, parts):
    return pl.pallas_call(
        views_kernel,
        out_shape=(
            jax.ShapeDtypeStruct((VIEWS, CR, STRIP), BF16),
            jax.ShapeDtypeStruct((CR, STRIP), BF16),
        ),
        in_specs=[SMEM] + [VMEM] * 4,
        out_specs=(VMEM,) * 2,
        compiler_params=PARAMS,
        name="all_views",
    )(pos, *parts)


def lane_places(width):
    lane = iota((1, width), 1) & (STRIP - 1)
    group = (lane >= GROUP).astype(I32) + (lane >= 2 * GROUP).astype(I32)
    return lane, group, lane - GROUP * group - HALO


def wrap_tiles(ref, size):
    lane = iota((1, STRIP), 1)
    last = ref[TILES * size : (TILES + 1) * size, :].astype(F32)
    first = ref[size : 2 * size, :].astype(F32)
    before = jnp.where(lane >= GROUP, pltpu.roll(last, GROUP, axis=1), 0.0)
    after = jnp.where(lane < 2 * GROUP, pltpu.roll(first, STRIP - GROUP, axis=1), 0.0)
    ref[0:size, :] = before.astype(BF16)
    ref[(TILES + 1) * size : (TILES + 2) * size, :] = after.astype(BF16)


def own_mask():
    lane, _, col = lane_places(STRIP)
    return ((col >= 0) & (col < OWN)).astype(F32)


def total_of(x):
    return jnp.sum(jnp.sum(x, axis=0, keepdims=True), axis=1, keepdims=True)


def conv_and_stats(w, ref, size, out, stats):
    mask = own_mask()

    def one(k, acc):
        rows = ref[pl.ds(pl.multiple_of(k * size, size), 3 * size), :]
        z = mm(w[...], rows)
        y = z[HR : 2 * HR] + pltpu.roll(z[:HR], 1, axis=1) + pltpu.roll(z[2 * HR :], STRIP - 1, axis=1)
        out[pl.ds(pl.multiple_of(k * HR, HR), HR), :] = y
        return acc + y

    acc = lax.fori_loop(0, TILES, one, jnp.zeros((HR, STRIP), F32), unroll=4) * mask
    means = [total_of(acc[ROWS * o : ROWS * (o + 1)]) * (1.0 / COUNT) for o in range(HID)]
    mean = jnp.concatenate([jnp.broadcast_to(m, (ROWS, STRIP)) for m in means], axis=0)

    def two(k, acc):
        dev = (out[pl.ds(pl.multiple_of(k * HR, HR), HR), :] - mean) * mask
        return acc + dev * dev

    acc = lax.fori_loop(0, TILES, two, jnp.zeros((HR, STRIP), F32), unroll=4)
    lane = iota((1, STRIP), 1)
    row = jnp.zeros((1, STRIP), F32)
    for o in range(HID):
        row = jnp.where(lane == o, means[o], row)
        row = jnp.where(lane == HID + o, total_of(acc[ROWS * o : ROWS * (o + 1)]), row)
    stats[...] = jnp.broadcast_to(row, (DEVICES, STRIP))


def normalized(pos, stats, values, act):
    lane = iota((1, STRIP), 1)
    rows = stats[...]
    center = jnp.sum(rows, axis=0, keepdims=True) * (1.0 / DEVICES)
    dev = rows - center
    between = jnp.sum(dev * dev, axis=0, keepdims=True)

    def pick(row, at):
        return jnp.sum(jnp.where(lane == at, row, 0.0), axis=1, keepdims=True)

    means, scales = [], []
    for o in range(HID):
        spread = pick(center, HID + o) * (1.0 / COUNT) + pick(between, o) * (1.0 / DEVICES)
        means.append(jnp.broadcast_to(pick(center, o), (ROWS, STRIP)))
        scales.append(jnp.broadcast_to(lax.rsqrt(spread + norm_eps), (ROWS, STRIP)))
    mean = jnp.concatenate(means, axis=0)
    scale = jnp.concatenate(scales, axis=0)
    _, _, col = lane_places(STRIP)
    col = col + (STRIP * pos[1] + OWN * pos[0])
    inside = (col >= 0) & (col < STRIP * pos[2])

    def one(k, carry):
        x = values[pl.ds(pl.multiple_of(k * HR, HR), HR), :]
        y = jnp.where(inside, jnp.maximum((x - mean) * scale, 0.0), 0.0)
        act[pl.ds(pl.multiple_of((k + 1) * HR, HR), HR), :] = y.astype(BF16)
        return carry

    lax.fori_loop(0, TILES, one, 0, unroll=4)
    wrap_tiles(act, HR)


def window_features(depth, every, left, edge, wf, feats):
    lane = iota((1, STRIP), 1)
    start = (OWN * depth + STRIP - EDGE) & (STRIP - 1)
    back = STRIP - start
    first = depth == 0

    def one(v, carry):
        own = every[v].astype(F32)
        before = left[v].astype(F32)
        far = pltpu.roll(edge[...].astype(F32), (3 * STRIP - EDGE * v - jnp.where(first, EDGE, 0)) & (STRIP - 1), axis=1)
        a = jnp.where(first, far, before)
        b = jnp.where(first, before, own)
        c = jnp.where(first, own, far)
        x = jnp.concatenate(
            [
                pltpu.roll(jnp.where(lane >= start, a, b), back, axis=1),
                pltpu.roll(jnp.where(lane >= start, b, c), back, axis=1),
            ],
            axis=1,
        ).astype(BF16)
        y = mm(wf[...], x)
        f = (
            y[CR : 2 * CR]
            + pltpu.roll(y[:CR], 1, axis=1)
            + pltpu.roll(y[2 * CR :], 2 * STRIP - 1, axis=1)
        )
        feats[v] = f.astype(BF16)
        return carry

    lax.fori_loop(0, VIEWS, one, 0)


def volume_kernel(pos, shifts, frame, every, left, edge, wf, w1, out, stats, feats, even, odd, vol):
    depth = pos[0]
    base = STRIP * pos[1] + OWN * depth
    wide = 2 * STRIP
    lane = iota((1, wide), 1)
    window_features(depth, every, left, edge, wf, feats)
    zero_view = pltpu.roll(feats[0].astype(F32), BASE - (LEFT - HALO), axis=1)
    own_lanes = (lane >= BASE) & (lane < BASE + GROUP)
    for v in range(1, VIEWS):
        feats[v] = jnp.where(own_lanes, zero_view, feats[v].astype(F32)).astype(BF16)

    _, group, col = lane_places(wide)
    half = lane >= STRIP
    glob = base + col
    valid = (glob >= 0) & (glob < STRIP * pos[2])
    places = iota((BASE, wide), 0)
    below = jnp.where(iota((wide - BASE, wide), 0) == col + HALO, -1.0, 0.0)

    def move(kk, moved):
        tally = jnp.ones((1, wide), F32)
        for v in range(1, VIEWS):
            at = [[shifts[v, TILES * j + 2 * kk + s] for j in range(3)] for s in range(2)]
            one, two = (
                jnp.where(group == 0, t[0], jnp.where(group == 1, t[1], t[2])) for t in at
            )
            shift = jnp.where(half, two, one)
            source = glob - shift
            inside = (source >= frame[v, 0]) & (source < frame[v, 1])
            index = jnp.where(inside, col - shift + LEFT, -1)
            hot = jnp.where(places == index, 1.0, 0.0).astype(BF16)
            mask = inside.astype(F32)
            hot = jnp.concatenate([hot, (below * mask).astype(BF16)], axis=0)
            moved[v - 1] = mm(feats[v], hot)
            tally = tally + mask
        return 1.0 / tally

    def spread(kk, moved, inverse):
        for r in range(0, CR, 16):
            total = squares = None
            for v in range(VIEWS - 1):
                p = moved[v, r : r + 16, :]
                total = p if total is None else total + p
                squares = p * p if squares is None else squares + p * p
            average = total * inverse
            value = jnp.where(valid, squares * inverse - average * average, 0.0)
            value = jnp.maximum(value, 0.0).astype(BF16)
            for s in range(2):
                row = pl.multiple_of((2 * kk + s + 1) * CR + r, 16)
                vol[pl.ds(row, 16), :] = value[:, s * STRIP : (s + 1) * STRIP]

    def step(t, inverse):
        spread(2 * t, even, inverse)
        later = move(2 * t + 1, odd)
        spread(2 * t + 1, odd, later)
        return move(jnp.minimum(2 * t + 2, TILES // 2 - 1), even)

    lax.fori_loop(0, TILES // 4, step, move(0, even))
    wrap_tiles(vol, CR)
    conv_and_stats(w1, vol, CR, out, stats)


def cost_and_conv(pos, shifts, frame, every, left, edge, wf, w1):
    return pl.pallas_call(
        volume_kernel,
        out_shape=(
            jax.ShapeDtypeStruct((TILES * HR, STRIP), F32),
            jax.ShapeDtypeStruct((DEVICES, STRIP), F32),
        ),
        in_specs=[SMEM] * 3 + [VMEM] * 5,
        out_specs=(VMEM,) * 2,
        scratch_shapes=[
            pltpu.VMEM((VIEWS, CR, 2 * STRIP), BF16),
            pltpu.VMEM((VIEWS - 1, CR, 2 * STRIP), F32),
            pltpu.VMEM((VIEWS - 1, CR, 2 * STRIP), F32),
            pltpu.VMEM(((TILES + 2) * CR, STRIP), BF16),
        ],
        compiler_params=PARAMS,
        name="cost_volume",
    )(pos, shifts, frame, every, left, edge, wf, w1)


def middle_kernel(pos, stats_in, values, w2, out, stats, act):
    normalized(pos, stats_in, values, act)
    conv_and_stats(w2, act, HR, out, stats)


def second_conv(pos, stats, values, w2):
    return pl.pallas_call(
        middle_kernel,
        out_shape=(
            jax.ShapeDtypeStruct((TILES * HR, STRIP), F32),
            jax.ShapeDtypeStruct((DEVICES, STRIP), F32),
        ),
        in_specs=[SMEM] + [VMEM] * 3,
        out_specs=(VMEM,) * 2,
        scratch_shapes=[pltpu.VMEM(((TILES + 2) * HR, STRIP), BF16)],
        compiler_params=PARAMS,
        name="second_conv",
    )(pos, stats, values, w2)


def last_kernel(pos, stats_in, values, w3, out, act, score):
    normalized(pos, stats_in, values, act)

    def one(k, peak):
        z = mm(w3[...], act[pl.ds(pl.multiple_of(k * HR, HR), 3 * HR), :])
        y = (
            z[ROWS : 2 * ROWS]
            + pltpu.roll(z[:ROWS], 1, axis=1)
            + pltpu.roll(z[2 * ROWS :], STRIP - 1, axis=1)
        )
        score[k] = y
        return jnp.maximum(peak, y)

    peak = lax.fori_loop(0, TILES, one, jnp.full((ROWS, STRIP), -jnp.inf, F32), unroll=4)
    _, group, _ = lane_places(STRIP)

    def two(k, sums):
        e = jnp.exp(score[k] - peak)
        value = (TILES * group + k).astype(F32) / (DEPTHS - 1)
        return sums[0] + e, sums[1] + e * value

    zero = jnp.zeros((ROWS, STRIP), F32)
    total, weighted = lax.fori_loop(0, TILES, two, (zero, zero), unroll=4)

    def turned(x):
        return [x] + [pltpu.roll(x, STRIP - j * GROUP, axis=1) for j in (1, 2)]

    peaks, totals, weights = turned(peak), turned(total), turned(weighted)
    top = jnp.maximum(jnp.maximum(peaks[0], peaks[1]), peaks[2])
    scales = [jnp.exp(p - top) for p in peaks]
    whole = sum(t * s for t, s in zip(totals, scales))
    mean = sum(t * s for t, s in zip(weights, scales)) / whole
    first = OWN * pos[0]
    lane = iota((1, STRIP), 1)
    moved = pltpu.roll(mean, (first + STRIP - HALO) & (STRIP - 1), axis=1)
    out[...] = jnp.where((lane >= first) & (lane < first + OWN), moved, 0.0)


def final_estimate(pos, stats, values, w3):
    return pl.pallas_call(
        last_kernel,
        out_shape=jax.ShapeDtypeStruct((ROWS, STRIP), F32),
        in_specs=[SMEM] + [VMEM] * 3,
        out_specs=VMEM,
        scratch_shapes=[
            pltpu.VMEM(((TILES + 2) * HR, STRIP), BF16),
            pltpu.VMEM((TILES, ROWS, STRIP), F32),
        ],
        compiler_params=PARAMS,
        name="final_estimate",
    )(pos, stats, values, w3)


def everyones(stats):
    return lax.all_to_all(stats, ("depth", "col"), 0, 0, tiled=True)


def local(raw_views, feat_weight, shifts, frame_range, cost_weight, mid_weight, final_weight):
    pos = jnp.stack([lax.axis_index("depth"), lax.axis_index("col"), jnp.int32(lax.axis_size("col"))])
    pos = pos.astype(I32)
    own = raw_views.reshape(2, CR, STRIP)
    with jax.named_scope("views"):
        parts = [own] + [lax.ppermute(own, "depth", [(i, i ^ k) for i in range(4)]) for k in (1, 2, 3)]
        every, edge = all_views(pos, parts)
    with jax.named_scope("strips"):
        cols = lax.axis_size("col")
        far = [(i, i + 2) for i in range(cols - 2)] + [(3 * cols + i, 3 * cols + i - 1) for i in range(1, cols)]
        left = lax.ppermute(every, "col", [(i, i + 1) for i in range(cols - 1)])
        edge = lax.ppermute(edge, ("depth", "col"), far)
    *weights, every = lax.optimization_barrier(
        (feat_weight, cost_weight, mid_weight, final_weight, every)
    )
    wf, w1, w2, w3 = make_weights(*weights)
    first, stats = cost_and_conv(pos, shifts, frame_range, every, left, edge, wf, w1)
    second, stats = second_conv(pos, everyones(stats), first, w2)
    part = final_estimate(pos, everyones(stats), second, w3)
    with jax.named_scope("columns"):
        others = [lax.ppermute(part, "depth", [(i, i ^ k) for i in range(4)]) for k in (1, 2, 3)]
        return part + others[0] + others[1] + others[2]


def solution(mesh):
    in_specs = (P("depth", None, None, "col"), P(), P(), P(), P(), P(), P())
    out_specs = P(None, "col")
    return jax.shard_map(local, mesh=mesh, in_specs=in_specs, out_specs=out_specs, check_vma=False)
```

```python
import jax
import jax.numpy as jnp
from jax import lax
from jax.experimental import pallas as pl
from jax.experimental.pallas import tpu as pltpu
from jax.sharding import PartitionSpec as P

norm_eps = 1e-05

F32 = jnp.float32
BF16 = jnp.bfloat16
I32 = jnp.int32

VIEWS = 8
CHAN = 32
HID = 8
ROWS = 8
DEPTHS = 96
STRIP = 128
OWN = 32
WIDE = 256
GROUP = 42
GROUPS = 6
BLOCKS = 16
HALO = 5
UNROLL = 16
LEFT = 136
EDGE = 8
BASE = 176
CR = CHAN * ROWS
HR = HID * ROWS
DEVICES = 256
COUNT = DEPTHS * ROWS * OWN

VMEM = pl.BlockSpec(memory_space=pltpu.VMEM)
SMEM = pl.BlockSpec(memory_space=pltpu.SMEM)
PARAMS = pltpu.CompilerParams(vmem_limit_bytes=48 * 1024 * 1024)


def iota(shape, axis):
    return lax.broadcasted_iota(I32, shape, axis)


def mm(a, b):
    return jnp.dot(a, b, preferred_element_type=F32)


def spread_rows(count):
    return ((iota((8 * count, count), 0) >> 3) == iota((8 * count, count), 1)).astype(F32).astype(BF16)


def spread_cols(count):
    return (iota((count, 8 * count), 0) == (iota((count, 8 * count), 1) >> 3)).astype(F32).astype(BF16)


def banded(taps, left, right):
    total = None
    for b, w in enumerate(taps):
        t = w if left is None else mm(left, w).astype(BF16)
        u = mm(t, right)
        rows, cols = u.shape
        band = ((iota((rows, cols), 1) & 7) - (iota((rows, cols), 0) & 7)) == (b - 1)
        u = jnp.where(band, u, 0.0)
        total = u if total is None else total + u
    return total


def weights_kernel(fw, cw, mw, lw, wf, w1, w2, w3):
    ro32, ro8 = spread_rows(CHAN), spread_rows(HID)
    ci32, ci8 = spread_cols(CHAN), spread_cols(HID)
    for b in range(3):
        wf[:, b * CR : (b + 1) * CR] = banded([fw[3 * a + b] for a in range(3)], ro32, ci32).astype(BF16)
    for a in range(3):
        for e in range(3):
            taps = [9 * a + 3 * b + e for b in range(3)]
            w1[e * HR : (e + 1) * HR, a * CR : (a + 1) * CR] = banded(
                [cw[t] for t in taps], ro8, ci32
            ).astype(BF16)
    second, last = [], []
    for e in range(3):
        row2, row3 = [], []
        for a in range(3):
            taps = [9 * a + 3 * b + e for b in range(3)]
            row2.append(banded([mw[t] for t in taps], ro8, ci8))
            row3.append(
                banded([jnp.broadcast_to(lw[t], (ROWS, HID)).astype(BF16) for t in taps], None, ci8)
            )
        second.append(jnp.concatenate(row2, axis=1))
        last.append(jnp.concatenate(row3, axis=1))
    w2[...] = jnp.concatenate(second, axis=0).astype(BF16)
    w3[...] = jnp.concatenate(last, axis=0).astype(BF16)


def make_weights(feat_weight, cost_weight, mid_weight, final_weight):
    return pl.pallas_call(
        weights_kernel,
        out_shape=(
            jax.ShapeDtypeStruct((CR, 3 * CR), BF16),
            jax.ShapeDtypeStruct((3 * HR, 3 * CR), BF16),
            jax.ShapeDtypeStruct((3 * HR, 3 * HR), BF16),
            jax.ShapeDtypeStruct((3 * ROWS, 3 * HR), BF16),
        ),
        in_specs=[VMEM] * 4,
        out_specs=(VMEM,) * 4,
        compiler_params=PARAMS,
        cost_estimate=pl.CostEstimate(flops=2_000_000_000, bytes_accessed=1_000_000, transcendentals=0),
        name="banded_weights",
    )(feat_weight, cost_weight, mid_weight, final_weight.astype(F32).reshape(27, 1, HID))


def views_kernel(pos, r0, r1, r2, r3, every, edge):
    depth = pos[0]
    for k, r in enumerate((r0, r1, r2, r3)):
        for u in range(2):
            every[2 * (depth ^ k) + u] = r[u]
    lane = iota((1, STRIP), 1)
    turn = jnp.where(depth == 0, EDGE, 0)
    packed = jnp.zeros((CR, STRIP), F32)
    for v in range(VIEWS):
        x = pltpu.roll(every[v].astype(F32), turn + EDGE * v, axis=1)
        packed = jnp.where((lane >> 3) == v, x, packed)
    edge[...] = packed.astype(BF16)


def copy_kernel(x, y):
    y[...] = x[...]


def copied(x):
    return pl.pallas_call(
        copy_kernel,
        out_shape=jax.ShapeDtypeStruct(x.shape, x.dtype),
        in_specs=[VMEM],
        out_specs=VMEM,
        compiler_params=PARAMS,
        name="own_strip",
    )(x)


def all_views(pos, parts):
    return pl.pallas_call(
        views_kernel,
        out_shape=(
            jax.ShapeDtypeStruct((VIEWS, CR, STRIP), BF16),
            jax.ShapeDtypeStruct((CR, STRIP), BF16),
        ),
        in_specs=[SMEM] + [VMEM] * 4,
        out_specs=(VMEM,) * 2,
        compiler_params=PARAMS,
        name="all_views",
    )(pos, *parts)


def lane_places():
    lane = iota((1, WIDE), 1)
    group = sum((lane >= GROUP * g).astype(I32) for g in range(1, GROUPS))
    return lane, group, lane - GROUP * group - HALO


def wrap_blocks(ref, size):
    lane = iota((1, WIDE), 1)
    last = ref[BLOCKS * size : (BLOCKS + 1) * size, :].astype(F32)
    first = ref[size : 2 * size, :].astype(F32)
    before = jnp.where(lane >= GROUP, pltpu.roll(last, GROUP, axis=1), 0.0)
    after = jnp.where(lane < (GROUPS - 1) * GROUP, pltpu.roll(first, WIDE - GROUP, axis=1), 0.0)
    ref[0:size, :] = before.astype(BF16)
    ref[(BLOCKS + 1) * size : (BLOCKS + 2) * size, :] = after.astype(BF16)


def total_of(x):
    return jnp.sum(jnp.sum(x, axis=0, keepdims=True), axis=1, keepdims=True)


def joined(z, rows):
    return (
        z[rows : 2 * rows]
        + pltpu.roll(z[:rows], 1, axis=1)
        + pltpu.roll(z[2 * rows :], WIDE - 1, axis=1)
    )


def conv_and_stats(w, ref, size, out, stats):
    _, _, col = lane_places()
    mine = (col >= 0) & (col < OWN)

    def one(k, acc):
        rows = ref[pl.ds(pl.multiple_of(k * size, size), 3 * size), :]
        y = joined(mm(w[...], rows), HR)
        out[pl.ds(pl.multiple_of(k * HR, HR), HR), :] = y
        return acc + y

    acc = lax.fori_loop(0, BLOCKS, one, jnp.zeros((HR, WIDE), F32), unroll=UNROLL)
    acc = jnp.where(mine, acc, 0.0)
    means = [total_of(acc[ROWS * o : ROWS * (o + 1)]) * (1.0 / COUNT) for o in range(HID)]
    mean = jnp.concatenate([jnp.broadcast_to(m, (ROWS, WIDE)) for m in means], axis=0)

    def two(k, acc):
        dev = out[pl.ds(pl.multiple_of(k * HR, HR), HR), :] - mean
        return acc + dev * dev

    acc = lax.fori_loop(0, BLOCKS, two, jnp.zeros((HR, WIDE), F32), unroll=2)
    acc = jnp.where(mine, acc, 0.0)
    lane = iota((1, STRIP), 1)
    row = jnp.zeros((1, STRIP), F32)
    for o in range(HID):
        row = jnp.where(lane == o, means[o], row)
        row = jnp.where(lane == HID + o, total_of(acc[ROWS * o : ROWS * (o + 1)]), row)
    stats[...] = jnp.broadcast_to(row, (DEVICES, STRIP))


def normalized(pos, stats, values, act):
    lane = iota((1, STRIP), 1)
    rows = stats[...]
    center = jnp.sum(rows, axis=0, keepdims=True) * (1.0 / DEVICES)
    dev = rows - center
    between = jnp.sum(dev * dev, axis=0, keepdims=True)

    def pick(row, at):
        return jnp.sum(jnp.where(lane == at, row, 0.0), axis=1, keepdims=True)

    means, scales = [], []
    for o in range(HID):
        spread = pick(center, HID + o) * (1.0 / COUNT) + pick(between, o) * (1.0 / DEVICES)
        means.append(jnp.broadcast_to(pick(center, o), (ROWS, WIDE)))
        scales.append(jnp.broadcast_to(lax.rsqrt(spread + norm_eps), (ROWS, WIDE)))
    mean = jnp.concatenate(means, axis=0)
    scale = jnp.concatenate(scales, axis=0)
    _, _, col = lane_places()
    col = col + (STRIP * pos[1] + OWN * pos[0])
    inside = (col >= 0) & (col < STRIP * pos[2])

    def one(k, carry):
        x = values[pl.ds(pl.multiple_of(k * HR, HR), HR), :]
        y = jnp.where(inside, jnp.maximum((x - mean) * scale, 0.0), 0.0)
        act[pl.ds(pl.multiple_of((k + 1) * HR, HR), HR), :] = y.astype(BF16)
        return carry

    lax.fori_loop(0, BLOCKS, one, 0, unroll=2)
    wrap_blocks(act, HR)


def window_features(depth, every, left, edge, wf, feats):
    lane = iota((1, STRIP), 1)
    start = (OWN * depth + STRIP - EDGE) & (STRIP - 1)
    first = depth == 0

    def one(v, carry):
        own = every[v].astype(F32)
        before = left[v].astype(F32)
        turn = (3 * STRIP - EDGE * v - jnp.where(first, EDGE, 0)) & (STRIP - 1)
        far = pltpu.roll(edge[...].astype(F32), turn, axis=1)
        a = jnp.where(first, far, before)
        b = jnp.where(first, before, own)
        c = jnp.where(first, own, far)
        taps = []
        for at in (start - 1, start, start + 1):
            one_half = pltpu.roll(jnp.where(lane >= at, a, b), STRIP - at, axis=1)
            two_half = pltpu.roll(jnp.where(lane >= at, b, c), STRIP - at, axis=1)
            taps.append(jnp.concatenate([one_half, two_half], axis=1).astype(BF16))
        feats[v] = mm(wf[...], jnp.concatenate(taps, axis=0)).astype(BF16)
        return carry

    lax.fori_loop(0, VIEWS, one, 0, unroll=8)


def volume_kernel(pos, shifts, frame, every, left, edge, wf, w1, out, stats, feats, even, odd, vol):
    depth = pos[0]
    base = STRIP * pos[1] + OWN * depth
    lane, group, col = lane_places()
    window_features(depth, every, left, edge, wf, feats)
    zero_view = pltpu.roll(feats[0].astype(F32), BASE - (LEFT - HALO), axis=1)
    own_lanes = (lane >= BASE) & (lane < BASE + GROUP)
    for v in range(1, VIEWS):
        feats[v] = jnp.where(own_lanes, zero_view, feats[v].astype(F32)).astype(BF16)

    glob = base + col
    valid = (glob >= 0) & (glob < STRIP * pos[2])
    places = iota((BASE, WIDE), 0).astype(F32).astype(BF16)
    below = jnp.where(iota((WIDE - BASE, WIDE), 0) == col + HALO, -1.0, 0.0).astype(BF16)
    ones = jnp.ones((BASE, WIDE), BF16)
    none = jnp.zeros((BASE, WIDE), BF16)

    def move(k, v, moved):
        shift = shifts[v, k]
        for g in range(1, GROUPS):
            shift = jnp.where(group == g, shifts[v, BLOCKS * g + k], shift)
        source = glob - shift
        inside = (source >= frame[v, 0]) & (source < frame[v, 1])
        index = jnp.where(inside, col - shift + LEFT, -1)
        index = jnp.broadcast_to(index.astype(F32), (16, WIDE)).astype(BF16)
        index = jnp.concatenate([index] * (BASE // 16), axis=0)
        hot = jnp.where(places == index, ones, none)
        mask = inside.astype(F32)
        packed = jnp.broadcast_to(mask, (16, WIDE)).astype(BF16)
        packed = jnp.concatenate([packed] * ((WIDE - BASE) // 16), axis=0)
        hot = jnp.concatenate([hot, below * packed], axis=0)
        moved[v - 1] = mm(feats[v], hot)
        return mask

    def spread(k, r, moved, inverse):
        total = squares = None
        for v in range(VIEWS - 1):
            p = moved[v, r : r + 16, :]
            total = p if total is None else total + p
            squares = p * p if squares is None else squares + p * p
        average = total * inverse
        value = jnp.where(valid, squares * inverse - average * average, 0.0)
        row = pl.multiple_of((k + 1) * CR + r, 16)
        vol[pl.ds(row, 16), :] = jnp.maximum(value, 0.0).astype(BF16)

    def both(k, into, moved, inverse):
        ahead = jnp.minimum(k + 1, BLOCKS - 1)
        tally = jnp.ones((1, WIDE), F32)
        chunks = CR // 16
        for v in range(1, VIEWS):
            tally = tally + move(ahead, v, into)
            for r in range(chunks * (v - 1) // (VIEWS - 1), chunks * v // (VIEWS - 1)):
                spread(k, 16 * r, moved, inverse)
        return 1.0 / tally

    tally = jnp.ones((1, WIDE), F32)
    for v in range(1, VIEWS):
        tally = tally + move(0, v, even)

    def step(t, inverse):
        return both(2 * t + 1, even, odd, both(2 * t, odd, even, inverse))

    lax.fori_loop(0, BLOCKS // 2, step, 1.0 / tally)
    wrap_blocks(vol, CR)
    conv_and_stats(w1, vol, CR, out, stats)


def cost_and_conv(pos, shifts, frame, every, left, edge, wf, w1):
    return pl.pallas_call(
        volume_kernel,
        out_shape=(
            jax.ShapeDtypeStruct((BLOCKS * HR, WIDE), F32),
            jax.ShapeDtypeStruct((DEVICES, STRIP), F32),
        ),
        in_specs=[SMEM] * 3 + [VMEM] * 5,
        out_specs=(VMEM,) * 2,
        scratch_shapes=[
            pltpu.VMEM((VIEWS, CR, WIDE), BF16),
            pltpu.VMEM((VIEWS - 1, CR, WIDE), F32),
            pltpu.VMEM((VIEWS - 1, CR, WIDE), F32),
            pltpu.VMEM(((BLOCKS + 2) * CR, WIDE), BF16),
        ],
        compiler_params=PARAMS,
        name="cost_volume",
    )(pos, shifts, frame, every, left, edge, wf, w1)


def middle_kernel(pos, stats_in, values, w2, out, stats, act):
    normalized(pos, stats_in, values, act)
    conv_and_stats(w2, act, HR, out, stats)


def second_conv(pos, stats, values, w2):
    return pl.pallas_call(
        middle_kernel,
        out_shape=(
            jax.ShapeDtypeStruct((BLOCKS * HR, WIDE), F32),
            jax.ShapeDtypeStruct((DEVICES, STRIP), F32),
        ),
        in_specs=[SMEM] + [VMEM] * 3,
        out_specs=(VMEM,) * 2,
        scratch_shapes=[pltpu.VMEM(((BLOCKS + 2) * HR, WIDE), BF16)],
        compiler_params=PARAMS,
        name="second_conv",
    )(pos, stats, values, w2)


def last_kernel(pos, stats_in, values, w3, out, act, score):
    normalized(pos, stats_in, values, act)

    def one(k, peak):
        y = joined(mm(w3[...], act[pl.ds(pl.multiple_of(k * HR, HR), 3 * HR), :]), ROWS)
        score[k] = y
        return jnp.maximum(peak, y)

    peak = lax.fori_loop(0, BLOCKS, one, jnp.full((ROWS, WIDE), -jnp.inf, F32), unroll=UNROLL)
    _, group, _ = lane_places()

    def two(k, sums):
        e = jnp.exp(score[k] - peak)
        value = (BLOCKS * group + k).astype(F32) / (DEPTHS - 1)
        return sums[0] + e, sums[1] + e * value

    zero = jnp.zeros((ROWS, WIDE), F32)
    total, weighted = lax.fori_loop(0, BLOCKS, two, (zero, zero), unroll=4)

    def turned(x):
        return [x[:, :STRIP]] + [
            pltpu.roll(x, WIDE - g * GROUP, axis=1)[:, :STRIP] for g in range(1, GROUPS)
        ]

    peaks, totals, weights = turned(peak), turned(total), turned(weighted)
    top = peaks[0]
    for p in peaks[1:]:
        top = jnp.maximum(top, p)
    scales = [jnp.exp(p - top) for p in peaks]
    whole = sum(t * s for t, s in zip(totals, scales))
    mean = sum(t * s for t, s in zip(weights, scales)) / whole
    first = OWN * pos[0]
    lane = iota((1, STRIP), 1)
    moved = pltpu.roll(mean, (first + STRIP - HALO) & (STRIP - 1), axis=1)
    out[...] = jnp.where((lane >= first) & (lane < first + OWN), moved, 0.0)


def final_estimate(pos, stats, values, w3):
    return pl.pallas_call(
        last_kernel,
        out_shape=jax.ShapeDtypeStruct((ROWS, STRIP), F32),
        in_specs=[SMEM] + [VMEM] * 3,
        out_specs=VMEM,
        scratch_shapes=[
            pltpu.VMEM(((BLOCKS + 2) * HR, WIDE), BF16),
            pltpu.VMEM((BLOCKS, ROWS, WIDE), F32),
        ],
        compiler_params=PARAMS,
        name="final_estimate",
    )(pos, stats, values, w3)


def everyones(stats):
    return lax.all_to_all(stats, ("depth", "col"), 0, 0, tiled=True)


def local(raw_views, feat_weight, shifts, frame_range, cost_weight, mid_weight, final_weight):
    pos = jnp.stack([lax.axis_index("depth"), lax.axis_index("col"), jnp.int32(lax.axis_size("col"))])
    pos = pos.astype(I32)
    own = raw_views.reshape(2, CR, STRIP)
    with jax.named_scope("views"):
        parts = [copied(own)] + [lax.ppermute(own, "depth", [(i, i ^ k) for i in range(4)]) for k in (1, 2, 3)]
        every, edge = all_views(pos, parts)
    with jax.named_scope("strips"):
        cols = lax.axis_size("col")
        far = [(i, i + 2) for i in range(cols - 2)] + [(3 * cols + i, 3 * cols + i - 1) for i in range(1, cols)]
        left = lax.ppermute(every, "col", [(i, i + 1) for i in range(cols - 1)])
        edge = lax.ppermute(edge, ("depth", "col"), far)
    *weights, every = lax.optimization_barrier(
        (feat_weight, cost_weight, mid_weight, final_weight, every)
    )
    wf, w1, w2, w3 = make_weights(*weights)
    first, stats = cost_and_conv(pos, shifts, frame_range, every, left, edge, wf, w1)
    second, stats = second_conv(pos, everyones(stats), first, w2)
    part = final_estimate(pos, everyones(stats), second, w3)
    with jax.named_scope("columns"):
        others = [lax.ppermute(part, "depth", [(i, i ^ k) for i in range(4)]) for k in (1, 2, 3)]
        return part + others[0] + others[1] + others[2]


def solution(mesh):
    in_specs = (P("depth", None, None, "col"), P(), P(), P(), P(), P(), P())
    out_specs = P(None, "col")
    return jax.shard_map(local, mesh=mesh, in_specs=in_specs, out_specs=out_specs, check_vma=False)
```

```python
import jax
import jax.numpy as jnp
from jax import lax
from jax.experimental import pallas as pl
from jax.experimental.pallas import tpu as pltpu
from jax.sharding import PartitionSpec as P

norm_eps = 1e-05

F32 = jnp.float32
BF16 = jnp.bfloat16
I32 = jnp.int32

VIEWS = 8
CHAN = 32
HID = 8
ROWS = 8
DEPTHS = 96
STRIP = 128
OWN = 32
WIDE = 256
GROUP = 42
GROUPS = 6
BLOCKS = 16
HALO = 5
UNROLL = 16
LEFT = 136
EDGE = 8
BASE = 176
CR = CHAN * ROWS
HR = HID * ROWS
DEVICES = 256
COUNT = DEPTHS * ROWS * OWN

VMEM = pl.BlockSpec(memory_space=pltpu.VMEM)
SMEM = pl.BlockSpec(memory_space=pltpu.SMEM)
PARAMS = pltpu.CompilerParams(vmem_limit_bytes=48 * 1024 * 1024)


def iota(shape, axis):
    return lax.broadcasted_iota(I32, shape, axis)


def mm(a, b):
    return jnp.dot(a, b, preferred_element_type=F32)


def spread_rows(count):
    return ((iota((8 * count, count), 0) >> 3) == iota((8 * count, count), 1)).astype(F32).astype(BF16)


def spread_cols(count):
    return (iota((count, 8 * count), 0) == (iota((count, 8 * count), 1) >> 3)).astype(F32).astype(BF16)


def bands(rows, cols):
    off = (iota((rows, cols), 1) & 7) - (iota((rows, cols), 0) & 7)
    return [off == b - 1 for b in range(3)]


def banded(places, parts):
    total = None
    for at, u in zip(places, parts):
        u = jnp.where(at, u, 0.0)
        total = u if total is None else total + u
    return total


def weights_kernel(fw, cw, mw, lw, wf, w1, w2, w3):
    ro32, ro8 = spread_rows(CHAN), spread_rows(HID)
    ci32, ci8 = spread_cols(CHAN), spread_cols(HID)
    feat, cost, mid, last = mm(fw[...], ci32), mm(cw[...], ci32), mm(mw[...], ci8), mm(lw[...], ci8)

    def rows_of(left, wide, tap, count):
        return mm(left, wide[count * tap : count * (tap + 1)].astype(BF16))

    places = bands(CR, CR)
    for b in range(3):
        parts = [rows_of(ro32, feat, 3 * a + b, CHAN) for a in range(3)]
        wf[:, b * CR : (b + 1) * CR] = banded(places, parts).astype(BF16)
    places = bands(HR, CR)
    for a in range(3):
        for e in range(3):
            parts = [rows_of(ro8, cost, 9 * a + 3 * b + e, HID) for b in range(3)]
            w1[e * HR : (e + 1) * HR, a * CR : (a + 1) * CR] = banded(places, parts).astype(BF16)
    places, few = bands(HR, HR), bands(ROWS, HR)
    second, third = [], []
    for e in range(3):
        row2, row3 = [], []
        for a in range(3):
            taps = [9 * a + 3 * b + e for b in range(3)]
            row2.append(banded(places, [rows_of(ro8, mid, t, HID) for t in taps]))
            row3.append(banded(few, [jnp.broadcast_to(last[t : t + 1], (ROWS, HR)) for t in taps]))
        second.append(jnp.concatenate(row2, axis=1))
        third.append(jnp.concatenate(row3, axis=1))
    w2[...] = jnp.concatenate(second, axis=0).astype(BF16)
    w3[...] = jnp.concatenate(third, axis=0).astype(BF16)


def make_weights(feat_weight, cost_weight, mid_weight, final_weight):
    return pl.pallas_call(
        weights_kernel,
        out_shape=(
            jax.ShapeDtypeStruct((CR, 3 * CR), BF16),
            jax.ShapeDtypeStruct((3 * HR, 3 * CR), BF16),
            jax.ShapeDtypeStruct((3 * HR, 3 * HR), BF16),
            jax.ShapeDtypeStruct((3 * ROWS, 3 * HR), BF16),
        ),
        in_specs=[VMEM] * 4,
        out_specs=(VMEM,) * 4,
        compiler_params=PARAMS,
        cost_estimate=pl.CostEstimate(flops=2_000_000_000, bytes_accessed=1_000_000, transcendentals=0),
        name="banded_weights",
    )(
        feat_weight.reshape(9 * CHAN, CHAN),
        cost_weight.reshape(27 * HID, CHAN),
        mid_weight.reshape(27 * HID, HID),
        final_weight,
    )


def views_kernel(pos, r0, r1, r2, r3, every, edge):
    depth = pos[0]
    for k, r in enumerate((r0, r1, r2, r3)):
        for u in range(2):
            every[2 * (depth ^ k) + u] = r[u]
    lane = iota((1, STRIP), 1)
    turn = jnp.where(depth == 0, EDGE, 0)
    packed = jnp.zeros((CR, STRIP), F32)
    for v in range(VIEWS):
        x = pltpu.roll(every[v].astype(F32), turn + EDGE * v, axis=1)
        packed = jnp.where((lane >> 3) == v, x, packed)
    edge[...] = packed.astype(BF16)


def copy_kernel(x, y):
    y[...] = x[...]


def copied(x):
    return pl.pallas_call(
        copy_kernel,
        out_shape=jax.ShapeDtypeStruct(x.shape, x.dtype),
        in_specs=[VMEM],
        out_specs=VMEM,
        compiler_params=PARAMS,
        name="own_strip",
    )(x)


def all_views(pos, parts):
    return pl.pallas_call(
        views_kernel,
        out_shape=(
            jax.ShapeDtypeStruct((VIEWS, CR, STRIP), BF16),
            jax.ShapeDtypeStruct((CR, STRIP), BF16),
        ),
        in_specs=[SMEM] + [VMEM] * 4,
        out_specs=(VMEM,) * 2,
        compiler_params=PARAMS,
        name="all_views",
    )(pos, *parts)


def lane_places():
    lane = iota((1, WIDE), 1)
    group = sum((lane >= GROUP * g).astype(I32) for g in range(1, GROUPS))
    return lane, group, lane - GROUP * group - HALO


def wrap_blocks(ref, size):
    lane = iota((1, WIDE), 1)
    last = ref[BLOCKS * size : (BLOCKS + 1) * size, :].astype(F32)
    first = ref[size : 2 * size, :].astype(F32)
    before = jnp.where(lane >= GROUP, pltpu.roll(last, GROUP, axis=1), 0.0)
    after = jnp.where(lane < (GROUPS - 1) * GROUP, pltpu.roll(first, WIDE - GROUP, axis=1), 0.0)
    ref[0:size, :] = before.astype(BF16)
    ref[(BLOCKS + 1) * size : (BLOCKS + 2) * size, :] = after.astype(BF16)


def total_of(x):
    return jnp.sum(jnp.sum(x, axis=0, keepdims=True), axis=1, keepdims=True)


def joined(z, rows):
    return (
        z[rows : 2 * rows]
        + pltpu.roll(z[:rows], 1, axis=1)
        + pltpu.roll(z[2 * rows :], WIDE - 1, axis=1)
    )


def conv_block(w, ref, size, out, k):
    rows = ref[k * size : (k + 3) * size, :]
    out[k * HR : (k + 1) * HR, :] = joined(mm(w[...], rows), HR)


def channel_stats(out, stats):
    _, _, col = lane_places()
    mine = (col >= 0) & (col < OWN)

    def one(k, acc):
        return acc + out[pl.ds(pl.multiple_of(k * HR, HR), HR), :]

    acc = lax.fori_loop(0, BLOCKS, one, jnp.zeros((HR, WIDE), F32), unroll=UNROLL)
    acc = jnp.where(mine, acc, 0.0)
    means = [total_of(acc[ROWS * o : ROWS * (o + 1)]) * (1.0 / COUNT) for o in range(HID)]
    mean = jnp.concatenate([jnp.broadcast_to(m, (ROWS, WIDE)) for m in means], axis=0)

    def two(k, acc):
        dev = out[pl.ds(pl.multiple_of(k * HR, HR), HR), :] - mean
        return acc + dev * dev

    acc = lax.fori_loop(0, BLOCKS, two, jnp.zeros((HR, WIDE), F32), unroll=UNROLL)
    acc = jnp.where(mine, acc, 0.0)
    lane = iota((1, STRIP), 1)
    row = jnp.zeros((1, STRIP), F32)
    for o in range(HID):
        row = jnp.where(lane == o, means[o], row)
        row = jnp.where(lane == HID + o, total_of(acc[ROWS * o : ROWS * (o + 1)]), row)
    stats[...] = jnp.broadcast_to(row, (DEVICES, STRIP))


def normalized(pos, stats, values, act):
    lane = iota((1, STRIP), 1)
    rows = stats[...]
    center = jnp.sum(rows, axis=0, keepdims=True) * (1.0 / DEVICES)
    dev = rows - center
    between = jnp.sum(dev * dev, axis=0, keepdims=True)

    def pick(row, at):
        return jnp.sum(jnp.where(lane == at, row, 0.0), axis=1, keepdims=True)

    means, scales = [], []
    for o in range(HID):
        spread = pick(center, HID + o) * (1.0 / COUNT) + pick(between, o) * (1.0 / DEVICES)
        means.append(jnp.broadcast_to(pick(center, o), (ROWS, WIDE)))
        scales.append(jnp.broadcast_to(lax.rsqrt(spread + norm_eps), (ROWS, WIDE)))
    mean = jnp.concatenate(means, axis=0)
    scale = jnp.concatenate(scales, axis=0)
    _, _, col = lane_places()
    col = col + (STRIP * pos[1] + OWN * pos[0])
    scale = jnp.where((col >= 0) & (col < STRIP * pos[2]), scale, 0.0)

    def one(k, carry):
        x = values[pl.ds(pl.multiple_of(k * HR, HR), HR), :]
        y = jnp.maximum((x - mean) * scale, 0.0)
        act[pl.ds(pl.multiple_of((k + 1) * HR, HR), HR), :] = y.astype(BF16)
        return carry

    lax.fori_loop(0, BLOCKS, one, 0, unroll=UNROLL)
    wrap_blocks(act, HR)


def window_features(depth, every, left, edge, wf, feats):
    lane = iota((1, STRIP), 1)
    start = (OWN * depth + STRIP - EDGE) & (STRIP - 1)
    first = depth == 0

    def one(v, carry):
        own = every[v].astype(F32)
        before = left[v].astype(F32)
        turn = (3 * STRIP - EDGE * v - jnp.where(first, EDGE, 0)) & (STRIP - 1)
        far = pltpu.roll(edge[...].astype(F32), turn, axis=1)
        a = jnp.where(first, far, before)
        b = jnp.where(first, before, own)
        c = jnp.where(first, own, far)
        taps = []
        for at in (start - 1, start, start + 1):
            one_half = pltpu.roll(jnp.where(lane >= at, a, b), STRIP - at, axis=1)
            two_half = pltpu.roll(jnp.where(lane >= at, b, c), STRIP - at, axis=1)
            taps.append(jnp.concatenate([one_half, two_half], axis=1).astype(BF16))
        feats[v] = mm(wf[...], jnp.concatenate(taps, axis=0)).astype(BF16)
        return carry

    lax.fori_loop(0, VIEWS, one, 0, unroll=8)


def volume_kernel(pos, shifts, frame, every, left, edge, wf, w1, out, stats, feats, even, odd, vol):
    depth = pos[0]
    base = STRIP * pos[1] + OWN * depth
    lane, group, col = lane_places()
    window_features(depth, every, left, edge, wf, feats)
    zero_view = pltpu.roll(feats[0].astype(F32), BASE - (LEFT - HALO), axis=1)
    own_lanes = (lane >= BASE) & (lane < BASE + GROUP)
    for v in range(1, VIEWS):
        feats[v] = jnp.where(own_lanes, zero_view, feats[v].astype(F32)).astype(BF16)

    glob = base + col
    valid = (glob >= 0) & (glob < STRIP * pos[2])
    places = iota((BASE, WIDE), 0).astype(F32).astype(BF16)
    below = jnp.where(iota((WIDE - BASE, WIDE), 0) == col + HALO, -1.0, 0.0).astype(BF16)
    ones = jnp.ones((BASE, WIDE), BF16)
    none = jnp.zeros((BASE, WIDE), BF16)

    def move(k, v, moved):
        shift = shifts[v, k]
        for g in range(1, GROUPS):
            shift = jnp.where(group == g, shifts[v, BLOCKS * g + k], shift)
        source = glob - shift
        inside = (source >= frame[v, 0]) & (source < frame[v, 1])
        index = jnp.where(inside, col - shift + LEFT, -1)
        index = jnp.broadcast_to(index.astype(F32), (16, WIDE)).astype(BF16)
        index = jnp.concatenate([index] * (BASE // 16), axis=0)
        hot = jnp.where(places == index, ones, none)
        mask = inside.astype(F32)
        packed = jnp.broadcast_to(mask, (16, WIDE)).astype(BF16)
        packed = jnp.concatenate([packed] * ((WIDE - BASE) // 16), axis=0)
        hot = jnp.concatenate([hot, below * packed], axis=0)
        moved[v - 1] = mm(feats[v], hot)
        return mask

    def spread(k, r, moved, inverse):
        total = squares = None
        for v in range(VIEWS - 1):
            p = moved[v, r : r + 16, :]
            total = p if total is None else total + p
            squares = p * p if squares is None else squares + p * p
        average = total * inverse
        value = squares * inverse - average * average
        row = (k + 1) * CR + r
        vol[row : row + 16, :] = jnp.maximum(value, 0.0).astype(BF16)

    def gathered(k, moved):
        tally = jnp.ones((1, WIDE), F32)
        for v in range(1, VIEWS):
            tally = tally + move(k, v, moved)
        return jnp.where(valid, 1.0 / tally, 0.0)

    inverse = gathered(0, even)
    for k in range(BLOCKS):
        here, there = (even, odd) if k % 2 == 0 else (odd, even)
        later = gathered(k + 1, there) if k + 1 < BLOCKS else None
        if k >= 3:
            conv_block(w1, vol, CR, out, k - 2)
        for r in range(CR // 16):
            spread(k, 16 * r, here, inverse)
        inverse = later
    wrap_blocks(vol, CR)
    for k in (0, BLOCKS - 2, BLOCKS - 1):
        conv_block(w1, vol, CR, out, k)
    channel_stats(out, stats)


def cost_and_conv(pos, shifts, frame, every, left, edge, wf, w1):
    return pl.pallas_call(
        volume_kernel,
        out_shape=(
            jax.ShapeDtypeStruct((BLOCKS * HR, WIDE), F32),
            jax.ShapeDtypeStruct((DEVICES, STRIP), F32),
        ),
        in_specs=[SMEM] * 3 + [VMEM] * 5,
        out_specs=(VMEM,) * 2,
        scratch_shapes=[
            pltpu.VMEM((VIEWS, CR, WIDE), BF16),
            pltpu.VMEM((VIEWS - 1, CR, WIDE), F32),
            pltpu.VMEM((VIEWS - 1, CR, WIDE), F32),
            pltpu.VMEM(((BLOCKS + 2) * CR, WIDE), BF16),
        ],
        compiler_params=PARAMS,
        name="cost_volume",
    )(pos, shifts, frame, every, left, edge, wf, w1)


def middle_kernel(pos, stats_in, values, w2, out, stats, act):
    normalized(pos, stats_in, values, act)
    for k in range(BLOCKS):
        conv_block(w2, act, HR, out, k)
    channel_stats(out, stats)


def second_conv(pos, stats, values, w2):
    return pl.pallas_call(
        middle_kernel,
        out_shape=(
            jax.ShapeDtypeStruct((BLOCKS * HR, WIDE), F32),
            jax.ShapeDtypeStruct((DEVICES, STRIP), F32),
        ),
        in_specs=[SMEM] + [VMEM] * 3,
        out_specs=(VMEM,) * 2,
        scratch_shapes=[pltpu.VMEM(((BLOCKS + 2) * HR, WIDE), BF16)],
        compiler_params=PARAMS,
        name="second_conv",
    )(pos, stats, values, w2)


def last_kernel(pos, stats_in, values, w3, out, act, score):
    normalized(pos, stats_in, values, act)

    def one(k, peak):
        y = joined(mm(w3[...], act[pl.ds(pl.multiple_of(k * HR, HR), 3 * HR), :]), ROWS)
        score[k] = y
        return jnp.maximum(peak, y)

    peak = lax.fori_loop(0, BLOCKS, one, jnp.full((ROWS, WIDE), -jnp.inf, F32), unroll=UNROLL)
    _, group, _ = lane_places()

    def two(k, sums):
        e = jnp.exp(score[k] - peak)
        value = (BLOCKS * group + k).astype(F32) / (DEPTHS - 1)
        return sums[0] + e, sums[1] + e * value

    zero = jnp.zeros((ROWS, WIDE), F32)
    total, weighted = lax.fori_loop(0, BLOCKS, two, (zero, zero), unroll=UNROLL)

    def turned(x):
        return [x[:, :STRIP]] + [
            pltpu.roll(x, WIDE - g * GROUP, axis=1)[:, :STRIP] for g in range(1, GROUPS)
        ]

    peaks, totals, weights = turned(peak), turned(total), turned(weighted)
    top = peaks[0]
    for p in peaks[1:]:
        top = jnp.maximum(top, p)
    scales = [jnp.exp(p - top) for p in peaks]
    whole = sum(t * s for t, s in zip(totals, scales))
    mean = sum(t * s for t, s in zip(weights, scales)) / whole
    first = OWN * pos[0]
    lane = iota((1, STRIP), 1)
    moved = pltpu.roll(mean, (first + STRIP - HALO) & (STRIP - 1), axis=1)
    out[...] = jnp.where((lane >= first) & (lane < first + OWN), moved, 0.0)


def final_estimate(pos, stats, values, w3):
    return pl.pallas_call(
        last_kernel,
        out_shape=jax.ShapeDtypeStruct((ROWS, STRIP), F32),
        in_specs=[SMEM] + [VMEM] * 3,
        out_specs=VMEM,
        scratch_shapes=[
            pltpu.VMEM(((BLOCKS + 2) * HR, WIDE), BF16),
            pltpu.VMEM((BLOCKS, ROWS, WIDE), F32),
        ],
        compiler_params=PARAMS,
        name="final_estimate",
    )(pos, stats, values, w3)


def everyones(stats):
    return lax.all_to_all(stats, ("depth", "col"), 0, 0, tiled=True)


def local(raw_views, feat_weight, shifts, frame_range, cost_weight, mid_weight, final_weight):
    pos = jnp.stack([lax.axis_index("depth"), lax.axis_index("col"), jnp.int32(lax.axis_size("col"))])
    pos = pos.astype(I32)
    own = raw_views.reshape(2, CR, STRIP)
    with jax.named_scope("views"):
        wf, w1, w2, w3 = make_weights(feat_weight, cost_weight, mid_weight, final_weight)
        parts = [copied(own)] + [lax.ppermute(own, "depth", [(i, i ^ k) for i in range(4)]) for k in (1, 2, 3)]
        wf, turned = lax.optimization_barrier((wf, pos))
        every, edge = all_views(turned, parts)
    with jax.named_scope("strips"):
        cols = lax.axis_size("col")
        far = [(i, i + 2) for i in range(cols - 2)] + [(3 * cols + i, 3 * cols + i - 1) for i in range(1, cols)]
        left = lax.ppermute(every, "col", [(i, i + 1) for i in range(cols - 1)])
        edge = lax.ppermute(edge, ("depth", "col"), far)
    first, stats = cost_and_conv(pos, shifts, frame_range, every, left, edge, wf, w1)
    second, stats = second_conv(pos, everyones(stats), first, w2)
    part = final_estimate(pos, everyones(stats), second, w3)
    with jax.named_scope("columns"):
        others = [lax.ppermute(part, "depth", [(i, i ^ k) for i in range(4)]) for k in (1, 2, 3)]
        return part + others[0] + others[1] + others[2]


def solution(mesh):
    in_specs = (P("depth", None, None, "col"), P(), P(), P(), P(), P(), P())
    out_specs = P(None, "col")
    return jax.shard_map(local, mesh=mesh, in_specs=in_specs, out_specs=out_specs, check_vma=False)
```

```python
import jax
import jax.numpy as jnp
from jax import lax
from jax.experimental import pallas as pl
from jax.experimental.pallas import tpu as pltpu
from jax.sharding import PartitionSpec as P

norm_eps = 1e-05

F32 = jnp.float32
BF16 = jnp.bfloat16
I32 = jnp.int32

VIEWS = 8
CHAN = 32
HID = 8
ROWS = 8
DEPTHS = 96
STRIP = 128
OWN = 32
WIDE = 256
GROUP = 42
GROUPS = 6
BLOCKS = 16
HALO = 5
UNROLL = 16
LEFT = 136
EDGE = 8
BASE = 176
CR = CHAN * ROWS
HR = HID * ROWS
DEVICES = 256
COUNT = DEPTHS * ROWS * OWN

VMEM = pl.BlockSpec(memory_space=pltpu.VMEM)
SMEM = pl.BlockSpec(memory_space=pltpu.SMEM)
PARAMS = pltpu.CompilerParams(vmem_limit_bytes=48 * 1024 * 1024)


def iota(shape, axis):
    return lax.broadcasted_iota(I32, shape, axis)


def mm(a, b):
    return jnp.dot(a, b, preferred_element_type=F32)


def spread_rows(count):
    return ((iota((8 * count, count), 0) >> 3) == iota((8 * count, count), 1)).astype(F32).astype(BF16)


def spread_cols(count):
    return (iota((count, 8 * count), 0) == (iota((count, 8 * count), 1) >> 3)).astype(F32).astype(BF16)


def bands(rows, cols):
    off = (iota((rows, cols), 1) & 7) - (iota((rows, cols), 0) & 7)
    return [off == b - 1 for b in range(3)]


def banded(places, parts):
    total = None
    for at, u in zip(places, parts):
        u = jnp.where(at, u, 0.0)
        total = u if total is None else total + u
    return total


def weights_kernel(fw, cw, mw, lw, wf, w1, w2, w3):
    ro32, ro8 = spread_rows(CHAN), spread_rows(HID)
    ci32, ci8 = spread_cols(CHAN), spread_cols(HID)
    feat, cost, mid, last = mm(fw[...], ci32), mm(cw[...], ci32), mm(mw[...], ci8), mm(lw[...], ci8)

    def rows_of(left, wide, tap, count):
        return mm(left, wide[count * tap : count * (tap + 1)].astype(BF16))

    places = bands(CR, CR)
    for b in range(3):
        parts = [rows_of(ro32, feat, 3 * a + b, CHAN) for a in range(3)]
        wf[:, b * CR : (b + 1) * CR] = banded(places, parts).astype(BF16)
    places = bands(HR, CR)
    for a in range(3):
        for e in range(3):
            parts = [rows_of(ro8, cost, 9 * a + 3 * b + e, HID) for b in range(3)]
            w1[e * HR : (e + 1) * HR, a * CR : (a + 1) * CR] = banded(places, parts).astype(BF16)
    places, few = bands(HR, HR), bands(ROWS, HR)
    second, third = [], []
    for e in range(3):
        row2, row3 = [], []
        for a in range(3):
            taps = [9 * a + 3 * b + e for b in range(3)]
            row2.append(banded(places, [rows_of(ro8, mid, t, HID) for t in taps]))
            row3.append(banded(few, [jnp.broadcast_to(last[t : t + 1], (ROWS, HR)) for t in taps]))
        second.append(jnp.concatenate(row2, axis=1))
        third.append(jnp.concatenate(row3, axis=1))
    w2[...] = jnp.concatenate(second, axis=0).astype(BF16)
    w3[...] = jnp.concatenate(third, axis=0).astype(BF16)


def make_weights(feat_weight, cost_weight, mid_weight, final_weight):
    return pl.pallas_call(
        weights_kernel,
        out_shape=(
            jax.ShapeDtypeStruct((CR, 3 * CR), BF16),
            jax.ShapeDtypeStruct((3 * HR, 3 * CR), BF16),
            jax.ShapeDtypeStruct((3 * HR, 3 * HR), BF16),
            jax.ShapeDtypeStruct((3 * ROWS, 3 * HR), BF16),
        ),
        in_specs=[VMEM] * 4,
        out_specs=(VMEM,) * 4,
        compiler_params=PARAMS,
        cost_estimate=pl.CostEstimate(flops=2_000_000_000, bytes_accessed=1_000_000, transcendentals=0),
        name="banded_weights",
    )(
        feat_weight.reshape(9 * CHAN, CHAN),
        cost_weight.reshape(27 * HID, CHAN),
        mid_weight.reshape(27 * HID, HID),
        final_weight,
    )


def views_kernel(pos, r0, r1, r2, r3, every):
    depth = pos[0]
    for k, r in enumerate((r0, r1, r2, r3)):
        for u in range(2):
            every[2 * (depth ^ k) + u] = r[u]


def edges_kernel(pos, every, edge):
    lane = iota((1, STRIP), 1)
    turn = jnp.where(pos[0] == 0, EDGE, 0)
    packed = jnp.zeros((CR, STRIP), F32)
    for v in range(VIEWS):
        x = pltpu.roll(every[v].astype(F32), turn + EDGE * v, axis=1)
        packed = jnp.where((lane >> 3) == v, x, packed)
    edge[...] = packed.astype(BF16)


def edges(pos, every):
    return pl.pallas_call(
        edges_kernel,
        out_shape=jax.ShapeDtypeStruct((CR, STRIP), BF16),
        in_specs=[SMEM, VMEM],
        out_specs=VMEM,
        compiler_params=PARAMS,
        name="edges",
    )(pos, every)


def copy_kernel(x, y):
    y[...] = x[...]


def copied(x):
    return pl.pallas_call(
        copy_kernel,
        out_shape=jax.ShapeDtypeStruct(x.shape, x.dtype),
        in_specs=[VMEM],
        out_specs=VMEM,
        compiler_params=PARAMS,
        name="own_strip",
    )(x)


def all_views(pos, parts):
    return pl.pallas_call(
        views_kernel,
        out_shape=jax.ShapeDtypeStruct((VIEWS, CR, STRIP), BF16),
        in_specs=[SMEM] + [VMEM] * 4,
        out_specs=VMEM,
        compiler_params=PARAMS,
        name="all_views",
    )(pos, *parts)


def lane_places():
    lane = iota((1, WIDE), 1)
    group = sum((lane >= GROUP * g).astype(I32) for g in range(1, GROUPS))
    return lane, group, lane - GROUP * group - HALO


def wrap_blocks(ref, size):
    lane = iota((1, WIDE), 1)
    last = ref[BLOCKS * size : (BLOCKS + 1) * size, :].astype(F32)
    first = ref[size : 2 * size, :].astype(F32)
    before = jnp.where(lane >= GROUP, pltpu.roll(last, GROUP, axis=1), 0.0)
    after = jnp.where(lane < (GROUPS - 1) * GROUP, pltpu.roll(first, WIDE - GROUP, axis=1), 0.0)
    ref[0:size, :] = before.astype(BF16)
    ref[(BLOCKS + 1) * size : (BLOCKS + 2) * size, :] = after.astype(BF16)


def total_of(x):
    return jnp.sum(jnp.sum(x, axis=0, keepdims=True), axis=1, keepdims=True)


def joined(z, rows):
    return (
        z[rows : 2 * rows]
        + pltpu.roll(z[:rows], 1, axis=1)
        + pltpu.roll(z[2 * rows :], WIDE - 1, axis=1)
    )


def conv_block(w, ref, size, out, k):
    rows = ref[k * size : (k + 3) * size, :]
    out[k * HR : (k + 1) * HR, :] = joined(mm(w[...], rows), HR)


def channel_stats(out, stats):
    _, _, col = lane_places()
    mine = (col >= 0) & (col < OWN)

    def one(k, acc):
        return acc + out[pl.ds(pl.multiple_of(k * HR, HR), HR), :]

    acc = lax.fori_loop(0, BLOCKS, one, jnp.zeros((HR, WIDE), F32), unroll=UNROLL)
    acc = jnp.where(mine, acc, 0.0)
    means = [total_of(acc[ROWS * o : ROWS * (o + 1)]) * (1.0 / COUNT) for o in range(HID)]
    mean = jnp.concatenate([jnp.broadcast_to(m, (ROWS, WIDE)) for m in means], axis=0)

    def two(k, acc):
        dev = out[pl.ds(pl.multiple_of(k * HR, HR), HR), :] - mean
        return acc + dev * dev

    acc = lax.fori_loop(0, BLOCKS, two, jnp.zeros((HR, WIDE), F32), unroll=UNROLL)
    acc = jnp.where(mine, acc, 0.0)
    lane = iota((1, STRIP), 1)
    row = jnp.zeros((1, STRIP), F32)
    for o in range(HID):
        row = jnp.where(lane == o, means[o], row)
        row = jnp.where(lane == HID + o, total_of(acc[ROWS * o : ROWS * (o + 1)]), row)
    stats[...] = jnp.broadcast_to(row, (DEVICES, STRIP))


def normalized(pos, stats, values, act):
    lane = iota((1, STRIP), 1)
    rows = stats[...]
    center = jnp.sum(rows, axis=0, keepdims=True) * (1.0 / DEVICES)
    dev = rows - center
    between = jnp.sum(dev * dev, axis=0, keepdims=True)

    def pick(row, at):
        return jnp.sum(jnp.where(lane == at, row, 0.0), axis=1, keepdims=True)

    means, scales = [], []
    for o in range(HID):
        spread = pick(center, HID + o) * (1.0 / COUNT) + pick(between, o) * (1.0 / DEVICES)
        means.append(jnp.broadcast_to(pick(center, o), (ROWS, WIDE)))
        scales.append(jnp.broadcast_to(lax.rsqrt(spread + norm_eps), (ROWS, WIDE)))
    mean = jnp.concatenate(means, axis=0)
    scale = jnp.concatenate(scales, axis=0)
    _, _, col = lane_places()
    col = col + (STRIP * pos[1] + OWN * pos[0])
    scale = jnp.where((col >= 0) & (col < STRIP * pos[2]), scale, 0.0)

    def one(k, carry):
        x = values[pl.ds(pl.multiple_of(k * HR, HR), HR), :]
        y = jnp.maximum((x - mean) * scale, 0.0)
        act[pl.ds(pl.multiple_of((k + 1) * HR, HR), HR), :] = y.astype(BF16)
        return carry

    lax.fori_loop(0, BLOCKS, one, 0, unroll=UNROLL)
    wrap_blocks(act, HR)


def window_features(depth, every, left, edge, wf, feats):
    lane = iota((1, STRIP), 1)
    start = (OWN * depth + STRIP - EDGE) & (STRIP - 1)
    first = depth == 0

    def one(v, carry):
        own = every[v].astype(F32)
        before = left[v].astype(F32)
        turn = (3 * STRIP - EDGE * v - jnp.where(first, EDGE, 0)) & (STRIP - 1)
        far = pltpu.roll(edge[...].astype(F32), turn, axis=1)
        a = jnp.where(first, far, before)
        b = jnp.where(first, before, own)
        c = jnp.where(first, own, far)
        taps = []
        for at in (start - 1, start, start + 1):
            one_half = pltpu.roll(jnp.where(lane >= at, a, b), STRIP - at, axis=1)
            two_half = pltpu.roll(jnp.where(lane >= at, b, c), STRIP - at, axis=1)
            taps.append(jnp.concatenate([one_half, two_half], axis=1).astype(BF16))
        feats[v] = mm(wf[...], jnp.concatenate(taps, axis=0)).astype(BF16)
        return carry

    lax.fori_loop(0, VIEWS, one, 0, unroll=8)


def volume_kernel(pos, shifts, frame, every, left, edge, wf, w1, out, stats, feats, even, odd, vol):
    depth = pos[0]
    base = STRIP * pos[1] + OWN * depth
    lane, group, col = lane_places()
    window_features(depth, every, left, edge, wf, feats)
    zero_view = pltpu.roll(feats[0].astype(F32), BASE - (LEFT - HALO), axis=1)
    own_lanes = (lane >= BASE) & (lane < BASE + GROUP)
    for v in range(1, VIEWS):
        feats[v] = jnp.where(own_lanes, zero_view, feats[v].astype(F32)).astype(BF16)

    glob = base + col
    valid = (glob >= 0) & (glob < STRIP * pos[2])
    places = iota((BASE, WIDE), 0).astype(F32).astype(BF16)
    below = jnp.where(iota((WIDE - BASE, WIDE), 0) == col + HALO, -1.0, 0.0).astype(BF16)
    ones = jnp.ones((BASE, WIDE), BF16)
    none = jnp.zeros((BASE, WIDE), BF16)

    def move(k, v, moved):
        shift = shifts[v, k]
        for g in range(1, GROUPS):
            shift = jnp.where(group == g, shifts[v, BLOCKS * g + k], shift)
        source = glob - shift
        inside = (source >= frame[v, 0]) & (source < frame[v, 1])
        index = jnp.where(inside, col - shift + LEFT, -1)
        index = jnp.broadcast_to(index.astype(F32), (16, WIDE)).astype(BF16)
        index = jnp.concatenate([index] * (BASE // 16), axis=0)
        hot = jnp.where(places == index, ones, none)
        mask = inside.astype(F32)
        packed = jnp.broadcast_to(mask, (16, WIDE)).astype(BF16)
        packed = jnp.concatenate([packed] * ((WIDE - BASE) // 16), axis=0)
        hot = jnp.concatenate([hot, below * packed], axis=0)
        moved[v - 1] = mm(feats[v], hot)
        return mask

    def spread(k, r, moved, inverse):
        total = squares = None
        for v in range(VIEWS - 1):
            p = moved[v, r : r + 16, :]
            total = p if total is None else total + p
            squares = p * p if squares is None else squares + p * p
        average = total * inverse
        value = squares * inverse - average * average
        row = (k + 1) * CR + r
        vol[row : row + 16, :] = jnp.maximum(value, 0.0).astype(BF16)

    def gathered(k, moved):
        tally = jnp.ones((1, WIDE), F32)
        for v in range(1, VIEWS):
            tally = tally + move(k, v, moved)
        return jnp.where(valid, 1.0 / tally, 0.0)

    inverse = gathered(0, even)
    for k in range(BLOCKS):
        here, there = (even, odd) if k % 2 == 0 else (odd, even)
        for r in range(CR // 16):
            spread(k, 16 * r, here, inverse)
        if k + 1 < BLOCKS:
            inverse = gathered(k + 1, there)
        if k >= 3:
            conv_block(w1, vol, CR, out, k - 2)
    wrap_blocks(vol, CR)
    for k in (0, BLOCKS - 2, BLOCKS - 1):
        conv_block(w1, vol, CR, out, k)
    channel_stats(out, stats)


def cost_and_conv(pos, shifts, frame, every, left, edge, wf, w1):
    return pl.pallas_call(
        volume_kernel,
        out_shape=(
            jax.ShapeDtypeStruct((BLOCKS * HR, WIDE), F32),
            jax.ShapeDtypeStruct((DEVICES, STRIP), F32),
        ),
        in_specs=[SMEM] * 3 + [VMEM] * 5,
        out_specs=(VMEM,) * 2,
        scratch_shapes=[
            pltpu.VMEM((VIEWS, CR, WIDE), BF16),
            pltpu.VMEM((VIEWS - 1, CR, WIDE), F32),
            pltpu.VMEM((VIEWS - 1, CR, WIDE), F32),
            pltpu.VMEM(((BLOCKS + 2) * CR, WIDE), BF16),
        ],
        compiler_params=PARAMS,
        name="cost_volume",
    )(pos, shifts, frame, every, left, edge, wf, w1)


def middle_kernel(pos, stats_in, values, w2, out, stats, act):
    normalized(pos, stats_in, values, act)
    for k in range(BLOCKS):
        conv_block(w2, act, HR, out, k)
    channel_stats(out, stats)


def second_conv(pos, stats, values, w2):
    return pl.pallas_call(
        middle_kernel,
        out_shape=(
            jax.ShapeDtypeStruct((BLOCKS * HR, WIDE), F32),
            jax.ShapeDtypeStruct((DEVICES, STRIP), F32),
        ),
        in_specs=[SMEM] + [VMEM] * 3,
        out_specs=(VMEM,) * 2,
        scratch_shapes=[pltpu.VMEM(((BLOCKS + 2) * HR, WIDE), BF16)],
        compiler_params=PARAMS,
        name="second_conv",
    )(pos, stats, values, w2)


def last_kernel(pos, stats_in, values, w3, out, act, score):
    normalized(pos, stats_in, values, act)

    def one(k, peak):
        y = joined(mm(w3[...], act[pl.ds(pl.multiple_of(k * HR, HR), 3 * HR), :]), ROWS)
        score[k] = y
        return jnp.maximum(peak, y)

    peak = lax.fori_loop(0, BLOCKS, one, jnp.full((ROWS, WIDE), -jnp.inf, F32), unroll=UNROLL)
    _, group, _ = lane_places()

    def two(k, sums):
        e = jnp.exp(score[k] - peak)
        value = (BLOCKS * group + k).astype(F32) / (DEPTHS - 1)
        return sums[0] + e, sums[1] + e * value

    zero = jnp.zeros((ROWS, WIDE), F32)
    total, weighted = lax.fori_loop(0, BLOCKS, two, (zero, zero), unroll=UNROLL)

    def turned(x):
        return [x[:, :STRIP]] + [
            pltpu.roll(x, WIDE - g * GROUP, axis=1)[:, :STRIP] for g in range(1, GROUPS)
        ]

    peaks, totals, weights = turned(peak), turned(total), turned(weighted)
    top = peaks[0]
    for p in peaks[1:]:
        top = jnp.maximum(top, p)
    scales = [jnp.exp(p - top) for p in peaks]
    whole = sum(t * s for t, s in zip(totals, scales))
    mean = sum(t * s for t, s in zip(weights, scales)) / whole
    first = OWN * pos[0]
    lane = iota((1, STRIP), 1)
    moved = pltpu.roll(mean, (first + STRIP - HALO) & (STRIP - 1), axis=1)
    out[...] = jnp.where((lane >= first) & (lane < first + OWN), moved, 0.0)


def final_estimate(pos, stats, values, w3):
    return pl.pallas_call(
        last_kernel,
        out_shape=jax.ShapeDtypeStruct((ROWS, STRIP), F32),
        in_specs=[SMEM] + [VMEM] * 3,
        out_specs=VMEM,
        scratch_shapes=[
            pltpu.VMEM(((BLOCKS + 2) * HR, WIDE), BF16),
            pltpu.VMEM((BLOCKS, ROWS, WIDE), F32),
        ],
        compiler_params=PARAMS,
        name="final_estimate",
    )(pos, stats, values, w3)


def everyones(stats):
    return lax.all_to_all(stats, ("depth", "col"), 0, 0, tiled=True)


def local(raw_views, feat_weight, shifts, frame_range, cost_weight, mid_weight, final_weight):
    pos = jnp.stack([lax.axis_index("depth"), lax.axis_index("col"), jnp.int32(lax.axis_size("col"))])
    pos = pos.astype(I32)
    own = raw_views.reshape(2, CR, STRIP)
    with jax.named_scope("views"):
        wf, w1, w2, w3 = make_weights(feat_weight, cost_weight, mid_weight, final_weight)
        parts = [copied(own)] + [lax.ppermute(own, "depth", [(i, i ^ k) for i in range(4)]) for k in (1, 2, 3)]
        wf, turned = lax.optimization_barrier((wf, pos))
        every = all_views(turned, parts)
    with jax.named_scope("strips"):
        cols = lax.axis_size("col")
        far = [(i, i + 2) for i in range(cols - 2)] + [(3 * cols + i, 3 * cols + i - 1) for i in range(1, cols)]
        left = lax.ppermute(every, "col", [(i, i + 1) for i in range(cols - 1)])
        edge = lax.ppermute(edges(pos, every), ("depth", "col"), far)
    first, stats = cost_and_conv(pos, shifts, frame_range, every, left, edge, wf, w1)
    second, stats = second_conv(pos, everyones(stats), first, w2)
    part = final_estimate(pos, everyones(stats), second, w3)
    with jax.named_scope("columns"):
        others = [lax.ppermute(part, "depth", [(i, i ^ k) for i in range(4)]) for k in (1, 2, 3)]
        return part + others[0] + others[1] + others[2]


def solution(mesh):
    in_specs = (P("depth", None, None, "col"), P(), P(), P(), P(), P(), P())
    out_specs = P(None, "col")
    return jax.shard_map(local, mesh=mesh, in_specs=in_specs, out_specs=out_specs, check_vma=False)
```

```python
import jax
import jax.numpy as jnp
from jax import lax
from jax.experimental import pallas as pl
from jax.experimental.pallas import tpu as pltpu
from jax.sharding import PartitionSpec as P

norm_eps = 1e-05

F32 = jnp.float32
BF16 = jnp.bfloat16
I32 = jnp.int32

VIEWS = 8
CHAN = 32
HID = 8
ROWS = 8
DEPTHS = 96
STRIP = 128
OWN = 32
WIDE = 256
GROUP = 42
GROUPS = 6
BLOCKS = 16
HALO = 5
UNROLL = 16
LEFT = 136
EDGE = 8
BASE = 176
CR = CHAN * ROWS
HR = HID * ROWS
DEVICES = 256
COUNT = DEPTHS * ROWS * OWN

VMEM = pl.BlockSpec(memory_space=pltpu.VMEM)
SMEM = pl.BlockSpec(memory_space=pltpu.SMEM)
PARAMS = pltpu.CompilerParams(vmem_limit_bytes=48 * 1024 * 1024)


def iota(shape, axis):
    return lax.broadcasted_iota(I32, shape, axis)


def mm(a, b):
    return jnp.dot(a, b, preferred_element_type=F32)


def spread_rows(count):
    return ((iota((8 * count, count), 0) >> 3) == iota((8 * count, count), 1)).astype(F32).astype(BF16)


def spread_cols(count):
    return (iota((count, 8 * count), 0) == (iota((count, 8 * count), 1) >> 3)).astype(F32).astype(BF16)


def bands(rows, cols):
    off = (iota((rows, cols), 1) & 7) - (iota((rows, cols), 0) & 7)
    return [off == b - 1 for b in range(3)]


def banded(places, parts):
    total = None
    for at, u in zip(places, parts):
        u = jnp.where(at, u, 0.0)
        total = u if total is None else total + u
    return total


def weights_kernel(fw, cw, mw, lw, wf, w1, w2, w3):
    ro32, ro8 = spread_rows(CHAN), spread_rows(HID)
    ci32, ci8 = spread_cols(CHAN), spread_cols(HID)
    feat, cost, mid, last = mm(fw[...], ci32), mm(cw[...], ci32), mm(mw[...], ci8), mm(lw[...], ci8)

    def rows_of(left, wide, tap, count):
        return mm(left, wide[count * tap : count * (tap + 1)].astype(BF16))

    places = bands(CR, CR)
    for b in range(3):
        parts = [rows_of(ro32, feat, 3 * a + b, CHAN) for a in range(3)]
        wf[:, b * CR : (b + 1) * CR] = banded(places, parts).astype(BF16)
    places = bands(HR, CR)
    for a in range(3):
        for e in range(3):
            parts = [rows_of(ro8, cost, 9 * a + 3 * b + e, HID) for b in range(3)]
            w1[e * HR : (e + 1) * HR, a * CR : (a + 1) * CR] = banded(places, parts).astype(BF16)
    places, few = bands(HR, HR), bands(ROWS, HR)
    second, third = [], []
    for e in range(3):
        row2, row3 = [], []
        for a in range(3):
            taps = [9 * a + 3 * b + e for b in range(3)]
            row2.append(banded(places, [rows_of(ro8, mid, t, HID) for t in taps]))
            row3.append(banded(few, [jnp.broadcast_to(last[t : t + 1], (ROWS, HR)) for t in taps]))
        second.append(jnp.concatenate(row2, axis=1))
        third.append(jnp.concatenate(row3, axis=1))
    w2[...] = jnp.concatenate(second, axis=0).astype(BF16)
    w3[...] = jnp.concatenate(third, axis=0).astype(BF16)


def make_weights(feat_weight, cost_weight, mid_weight, final_weight):
    return pl.pallas_call(
        weights_kernel,
        out_shape=(
            jax.ShapeDtypeStruct((CR, 3 * CR), BF16),
            jax.ShapeDtypeStruct((3 * HR, 3 * CR), BF16),
            jax.ShapeDtypeStruct((3 * HR, 3 * HR), BF16),
            jax.ShapeDtypeStruct((3 * ROWS, 3 * HR), BF16),
        ),
        in_specs=[VMEM] * 4,
        out_specs=(VMEM,) * 4,
        compiler_params=PARAMS,
        cost_estimate=pl.CostEstimate(flops=2_000_000_000, bytes_accessed=1_000_000, transcendentals=0),
        name="banded_weights",
    )(
        feat_weight.reshape(9 * CHAN, CHAN),
        cost_weight.reshape(27 * HID, CHAN),
        mid_weight.reshape(27 * HID, HID),
        final_weight,
    )


def views_kernel(pos, r0, r1, r2, r3, every):
    depth = pos[0]
    for k, r in enumerate((r0, r1, r2, r3)):
        for u in range(2):
            every[2 * (depth ^ k) + u] = r[u]


def edges_kernel(pos, every, edge):
    lane = iota((1, STRIP), 1)
    turn = jnp.where(pos[0] == 0, EDGE, 0)
    packed = jnp.zeros((CR, STRIP), F32)
    for v in range(VIEWS):
        x = pltpu.roll(every[v].astype(F32), turn + EDGE * v, axis=1)
        packed = jnp.where((lane >> 3) == v, x, packed)
    edge[...] = packed.astype(BF16)


def edges(pos, every):
    return pl.pallas_call(
        edges_kernel,
        out_shape=jax.ShapeDtypeStruct((CR, STRIP), BF16),
        in_specs=[SMEM, VMEM],
        out_specs=VMEM,
        compiler_params=PARAMS,
        name="edges",
    )(pos, every)


def copy_kernel(x, y):
    y[...] = x[...]


def copied(x):
    return pl.pallas_call(
        copy_kernel,
        out_shape=jax.ShapeDtypeStruct(x.shape, x.dtype),
        in_specs=[VMEM],
        out_specs=VMEM,
        compiler_params=PARAMS,
        name="own_strip",
    )(x)


def all_views(pos, parts):
    return pl.pallas_call(
        views_kernel,
        out_shape=jax.ShapeDtypeStruct((VIEWS, CR, STRIP), BF16),
        in_specs=[SMEM] + [VMEM] * 4,
        out_specs=VMEM,
        compiler_params=PARAMS,
        name="all_views",
    )(pos, *parts)


def lane_places():
    lane = iota((1, WIDE), 1)
    group = sum((lane >= GROUP * g).astype(I32) for g in range(1, GROUPS))
    return lane, group, lane - GROUP * group - HALO


def wrap_blocks(ref, size):
    lane = iota((1, WIDE), 1)
    last = ref[BLOCKS * size : (BLOCKS + 1) * size, :].astype(F32)
    first = ref[size : 2 * size, :].astype(F32)
    before = jnp.where(lane >= GROUP, pltpu.roll(last, GROUP, axis=1), 0.0)
    after = jnp.where(lane < (GROUPS - 1) * GROUP, pltpu.roll(first, WIDE - GROUP, axis=1), 0.0)
    ref[0:size, :] = before.astype(BF16)
    ref[(BLOCKS + 1) * size : (BLOCKS + 2) * size, :] = after.astype(BF16)


def total_of(x):
    return jnp.sum(jnp.sum(x, axis=0, keepdims=True), axis=1, keepdims=True)


def joined(z, rows):
    return (
        z[rows : 2 * rows]
        + pltpu.roll(z[:rows], 1, axis=1)
        + pltpu.roll(z[2 * rows :], WIDE - 1, axis=1)
    )


def conv_block(w, ref, size, out, k):
    rows = ref[k * size : (k + 3) * size, :]
    out[k * HR : (k + 1) * HR, :] = joined(mm(w[...], rows), HR)


def channel_stats(out, stats):
    _, _, col = lane_places()
    mine = (col >= 0) & (col < OWN)

    def one(k, acc):
        return acc + out[pl.ds(pl.multiple_of(k * HR, HR), HR), :]

    acc = lax.fori_loop(0, BLOCKS, one, jnp.zeros((HR, WIDE), F32), unroll=UNROLL)
    acc = jnp.where(mine, acc, 0.0)
    means = [total_of(acc[ROWS * o : ROWS * (o + 1)]) * (1.0 / COUNT) for o in range(HID)]
    mean = jnp.concatenate([jnp.broadcast_to(m, (ROWS, WIDE)) for m in means], axis=0)

    def two(k, acc):
        dev = out[pl.ds(pl.multiple_of(k * HR, HR), HR), :] - mean
        return acc + dev * dev

    acc = lax.fori_loop(0, BLOCKS, two, jnp.zeros((HR, WIDE), F32), unroll=UNROLL)
    acc = jnp.where(mine, acc, 0.0)
    lane = iota((1, STRIP), 1)
    row = jnp.zeros((1, STRIP), F32)
    for o in range(HID):
        row = jnp.where(lane == o, means[o], row)
        row = jnp.where(lane == HID + o, total_of(acc[ROWS * o : ROWS * (o + 1)]), row)
    stats[...] = jnp.broadcast_to(row, (DEVICES, STRIP))


def normalized(pos, stats, values, act):
    lane = iota((1, STRIP), 1)
    rows = stats[...]
    center = jnp.sum(rows, axis=0, keepdims=True) * (1.0 / DEVICES)
    dev = rows - center
    between = jnp.sum(dev * dev, axis=0, keepdims=True)

    def pick(row, at):
        return jnp.sum(jnp.where(lane == at, row, 0.0), axis=1, keepdims=True)

    means, scales = [], []
    for o in range(HID):
        spread = pick(center, HID + o) * (1.0 / COUNT) + pick(between, o) * (1.0 / DEVICES)
        means.append(jnp.broadcast_to(pick(center, o), (ROWS, WIDE)))
        scales.append(jnp.broadcast_to(lax.rsqrt(spread + norm_eps), (ROWS, WIDE)))
    mean = jnp.concatenate(means, axis=0)
    scale = jnp.concatenate(scales, axis=0)
    _, _, col = lane_places()
    col = col + (STRIP * pos[1] + OWN * pos[0])
    scale = jnp.where((col >= 0) & (col < STRIP * pos[2]), scale, 0.0)

    def one(k, carry):
        x = values[pl.ds(pl.multiple_of(k * HR, HR), HR), :]
        y = jnp.maximum((x - mean) * scale, 0.0)
        act[pl.ds(pl.multiple_of((k + 1) * HR, HR), HR), :] = y.astype(BF16)
        return carry

    lax.fori_loop(0, BLOCKS, one, 0, unroll=UNROLL)
    wrap_blocks(act, HR)


def window_features(depth, every, left, edge, wf, feats):
    lane = iota((1, STRIP), 1)
    start = (OWN * depth + STRIP - EDGE) & (STRIP - 1)
    first = depth == 0

    def one(v, carry):
        own = every[v].astype(F32)
        before = left[v].astype(F32)
        turn = (3 * STRIP - EDGE * v - jnp.where(first, EDGE, 0)) & (STRIP - 1)
        far = pltpu.roll(edge[...].astype(F32), turn, axis=1)
        a = jnp.where(first, far, before)
        b = jnp.where(first, before, own)
        c = jnp.where(first, own, far)
        taps = []
        for at in (start - 1, start, start + 1):
            one_half = pltpu.roll(jnp.where(lane >= at, a, b), STRIP - at, axis=1)
            two_half = pltpu.roll(jnp.where(lane >= at, b, c), STRIP - at, axis=1)
            taps.append(jnp.concatenate([one_half, two_half], axis=1).astype(BF16))
        feats[v] = mm(wf[...], jnp.concatenate(taps, axis=0)).astype(BF16)
        return carry

    lax.fori_loop(0, VIEWS, one, 0, unroll=8)


def volume_kernel(pos, shifts, frame, every, left, edge, wf, w1, out, stats, feats, even, odd, vol):
    depth = pos[0]
    base = STRIP * pos[1] + OWN * depth
    lane, group, col = lane_places()
    window_features(depth, every, left, edge, wf, feats)
    zero_view = pltpu.roll(feats[0].astype(F32), BASE - (LEFT - HALO), axis=1)
    own_lanes = (lane >= BASE) & (lane < BASE + GROUP)
    for v in range(1, VIEWS):
        feats[v] = jnp.where(own_lanes, zero_view, feats[v].astype(F32)).astype(BF16)

    glob = base + col
    valid = (glob >= 0) & (glob < STRIP * pos[2])
    places = iota((BASE, WIDE), 0).astype(F32).astype(BF16)
    below = jnp.where(iota((WIDE - BASE, WIDE), 0) == col + HALO, -1.0, 0.0).astype(BF16)
    ones = jnp.ones((BASE, WIDE), BF16)
    none = jnp.zeros((BASE, WIDE), BF16)

    def move(k, v, moved):
        shift = shifts[v, k]
        for g in range(1, GROUPS):
            shift = jnp.where(group == g, shifts[v, BLOCKS * g + k], shift)
        source = glob - shift
        inside = (source >= frame[v, 0]) & (source < frame[v, 1])
        index = jnp.where(inside, col - shift + LEFT, -1)
        index = jnp.broadcast_to(index.astype(F32), (16, WIDE)).astype(BF16)
        index = jnp.concatenate([index] * (BASE // 16), axis=0)
        hot = jnp.where(places == index, ones, none)
        mask = inside.astype(F32)
        packed = jnp.broadcast_to(mask, (16, WIDE)).astype(BF16)
        packed = jnp.concatenate([packed] * ((WIDE - BASE) // 16), axis=0)
        hot = jnp.concatenate([hot, below * packed], axis=0)
        moved[v - 1] = mm(feats[v], hot)
        return mask

    def spread(k, r, moved, inverse):
        total = squares = None
        for v in range(VIEWS - 1):
            p = moved[v, r : r + 32, :]
            total = p if total is None else total + p
            squares = p * p if squares is None else squares + p * p
        average = total * inverse
        value = squares * inverse - average * average
        row = (k + 1) * CR + r
        vol[row : row + 32, :] = jnp.maximum(value, 0.0).astype(BF16)

    def gathered(k, moved):
        tally = jnp.ones((1, WIDE), F32)
        for v in range(1, VIEWS):
            tally = tally + move(k, v, moved)
        return jnp.where(valid, 1.0 / tally, 0.0)

    inverse = gathered(0, even)
    for k in range(BLOCKS):
        here, there = (even, odd) if k % 2 == 0 else (odd, even)
        for r in range(CR // 32):
            spread(k, 32 * r, here, inverse)
        if k + 1 < BLOCKS:
            inverse = gathered(k + 1, there)
        if k >= 3:
            conv_block(w1, vol, CR, out, k - 2)
    wrap_blocks(vol, CR)
    for k in (0, BLOCKS - 2, BLOCKS - 1):
        conv_block(w1, vol, CR, out, k)
    channel_stats(out, stats)


def cost_and_conv(pos, shifts, frame, every, left, edge, wf, w1):
    return pl.pallas_call(
        volume_kernel,
        out_shape=(
            jax.ShapeDtypeStruct((BLOCKS * HR, WIDE), F32),
            jax.ShapeDtypeStruct((DEVICES, STRIP), F32),
        ),
        in_specs=[SMEM] * 3 + [VMEM] * 5,
        out_specs=(VMEM,) * 2,
        scratch_shapes=[
            pltpu.VMEM((VIEWS, CR, WIDE), BF16),
            pltpu.VMEM((VIEWS - 1, CR, WIDE), F32),
            pltpu.VMEM((VIEWS - 1, CR, WIDE), F32),
            pltpu.VMEM(((BLOCKS + 2) * CR, WIDE), BF16),
        ],
        compiler_params=PARAMS,
        name="cost_volume",
    )(pos, shifts, frame, every, left, edge, wf, w1)


def middle_kernel(pos, stats_in, values, w2, out, stats, act):
    normalized(pos, stats_in, values, act)
    for k in range(BLOCKS):
        conv_block(w2, act, HR, out, k)
    channel_stats(out, stats)


def second_conv(pos, stats, values, w2):
    return pl.pallas_call(
        middle_kernel,
        out_shape=(
            jax.ShapeDtypeStruct((BLOCKS * HR, WIDE), F32),
            jax.ShapeDtypeStruct((DEVICES, STRIP), F32),
        ),
        in_specs=[SMEM] + [VMEM] * 3,
        out_specs=(VMEM,) * 2,
        scratch_shapes=[pltpu.VMEM(((BLOCKS + 2) * HR, WIDE), BF16)],
        compiler_params=PARAMS,
        name="second_conv",
    )(pos, stats, values, w2)


def last_kernel(pos, stats_in, values, w3, out, act, score):
    normalized(pos, stats_in, values, act)

    def one(k, peak):
        y = joined(mm(w3[...], act[pl.ds(pl.multiple_of(k * HR, HR), 3 * HR), :]), ROWS)
        score[k] = y
        return jnp.maximum(peak, y)

    peak = lax.fori_loop(0, BLOCKS, one, jnp.full((ROWS, WIDE), -jnp.inf, F32), unroll=UNROLL)
    _, group, _ = lane_places()

    def two(k, sums):
        e = jnp.exp(score[k] - peak)
        value = (BLOCKS * group + k).astype(F32) / (DEPTHS - 1)
        return sums[0] + e, sums[1] + e * value

    zero = jnp.zeros((ROWS, WIDE), F32)
    total, weighted = lax.fori_loop(0, BLOCKS, two, (zero, zero), unroll=UNROLL)

    def turned(x):
        return [x[:, :STRIP]] + [
            pltpu.roll(x, WIDE - g * GROUP, axis=1)[:, :STRIP] for g in range(1, GROUPS)
        ]

    peaks, totals, weights = turned(peak), turned(total), turned(weighted)
    top = peaks[0]
    for p in peaks[1:]:
        top = jnp.maximum(top, p)
    scales = [jnp.exp(p - top) for p in peaks]
    whole = sum(t * s for t, s in zip(totals, scales))
    mean = sum(t * s for t, s in zip(weights, scales)) / whole
    first = OWN * pos[0]
    lane = iota((1, STRIP), 1)
    moved = pltpu.roll(mean, (first + STRIP - HALO) & (STRIP - 1), axis=1)
    out[...] = jnp.where((lane >= first) & (lane < first + OWN), moved, 0.0)


def final_estimate(pos, stats, values, w3):
    return pl.pallas_call(
        last_kernel,
        out_shape=jax.ShapeDtypeStruct((ROWS, STRIP), F32),
        in_specs=[SMEM] + [VMEM] * 3,
        out_specs=VMEM,
        scratch_shapes=[
            pltpu.VMEM(((BLOCKS + 2) * HR, WIDE), BF16),
            pltpu.VMEM((BLOCKS, ROWS, WIDE), F32),
        ],
        compiler_params=PARAMS,
        name="final_estimate",
    )(pos, stats, values, w3)


def everyones(stats):
    return lax.all_to_all(stats, ("depth", "col"), 0, 0, tiled=True)


def local(raw_views, feat_weight, shifts, frame_range, cost_weight, mid_weight, final_weight):
    pos = jnp.stack([lax.axis_index("depth"), lax.axis_index("col"), jnp.int32(lax.axis_size("col"))])
    pos = pos.astype(I32)
    own = raw_views.reshape(2, CR, STRIP)
    with jax.named_scope("views"):
        wf, w1, w2, w3 = make_weights(feat_weight, cost_weight, mid_weight, final_weight)
        parts = [copied(own)] + [lax.ppermute(own, "depth", [(i, i ^ k) for i in range(4)]) for k in (1, 2, 3)]
        wf, turned = lax.optimization_barrier((wf, pos))
        every = all_views(turned, parts)
    with jax.named_scope("strips"):
        cols = lax.axis_size("col")
        far = [(i, i + 2) for i in range(cols - 2)] + [(3 * cols + i, 3 * cols + i - 1) for i in range(1, cols)]
        left = lax.ppermute(every, "col", [(i, i + 1) for i in range(cols - 1)])
        edge = lax.ppermute(edges(pos, every), ("depth", "col"), far)
    first, stats = cost_and_conv(pos, shifts, frame_range, every, left, edge, wf, w1)
    second, stats = second_conv(pos, everyones(stats), first, w2)
    part = final_estimate(pos, everyones(stats), second, w3)
    with jax.named_scope("columns"):
        others = [lax.ppermute(part, "depth", [(i, i ^ k) for i in range(4)]) for k in (1, 2, 3)]
        return part + others[0] + others[1] + others[2]


def solution(mesh):
    in_specs = (P("depth", None, None, "col"), P(), P(), P(), P(), P(), P())
    out_specs = P(None, "col")
    return jax.shard_map(local, mesh=mesh, in_specs=in_specs, out_specs=out_specs, check_vma=False)
```
